32 devices in a mesh: angle: 4 (over y, x), gz: 8 (over z, core).
Axes of the slice: x: 2, y: 2, z: 4, core: 2. Of those that a mesh axis runs over, the one named last changes fastest.
Arguments:
- volume: bfloat16 [8, 512, 512], P('gz'), may hold values from -0.3984375 to 0.3984375
- probe: float32 [8, 2, 128, 128], replicated, may hold values from -0.046875 to 0.046875
- measured: float32 [4, 8, 128, 128], P('angle', 'gz'), may hold values from 2 to 40
- angle_index: int32 [4], P('angle'), may hold values from 0 to 3, each once
- row_offset: int32 [4, 8], P('angle', 'gz'), may hold values from -64 to -56, as said below
- col_offset: int32 [4, 8], P('angle', 'gz'), may hold values from 0 to 384, as said below
Outputs:
- volume_update: float32 [8, 512, 512], P('gz', 'angle')
- probe_update: float32 [8, 2, 128, 128], replicated
The draws below stay inside these ranges and needn't reach their ends.
Inputs may be any that keep to these rules, and one draw needn't show every extreme that they name: `row_offset`: windows may reach 64 rows past either end of the projection; both ends are used. `col_offset`: both ends are used. `angle_index`: each angle number once.
All inputs are finite; a program needn't handle non-finite values.
Results may differ from the reference program's by a relative error of at most 0.0005.
Values sent between devices are 32-bit elements; how exact they have to be, the bound alone decides.
A program may use at most 64 MiB of HBM per device.

```python
import math
import jax
import jax.numpy as jnp
from jax import lax

NX = 512
NY = 512
WIN = 128
MODES = 8
NZ = 8
ANGLES = 4
POS = 8


def draw_row_offset(key, part):
    key = jax.random.fold_in(key, 11)
    half = WIN // 2
    values = jax.random.randint(key, (ANGLES, POS), -half, NZ - half + 1)
    values = values.at[0, 0].set(NZ - half)
    return values.at[ANGLES - 1, POS - 1].set(-half)


def draw_col_offset(key, part):
    key = jax.random.fold_in(key, 23)
    values = jax.random.randint(key, (ANGLES, POS), 0, NY - WIN + 1)
    values = values.at[1, 0].set(NY - WIN)
    return values.at[ANGLES - 2, POS - 1].set(0)


def block_levels(rng, shape, shards, least, largest):
    gain, own = 1.0, jax.random.fold_in(rng, 6)
    for dim, shards_of in shards:
        heights = jnp.exp(jax.random.uniform(jax.random.fold_in(own, dim), (shards_of,), jnp.float32, least / len(shards), largest / len(shards)))
        gain = gain * jnp.repeat(heights, shape[dim] // shards_of).reshape([-1 if axis == dim else 1 for axis in range(len(shape))])
    return gain


def noise(stream_key, extent, scale, reach, shards=(), kind=jnp.bfloat16):
    loudness = block_levels(stream_key, extent, shards, -0.22, 0.18) if shards else 1.0
    drawn = jax.random.normal(stream_key, extent, jnp.float32) * scale * loudness
    return jnp.minimum(jnp.maximum(drawn, -reach), reach).astype(kind)


def setup_inputs(seed: int = 0) -> dict:
    seeds = jax.random.split(jax.random.key(seed), 7)
    volume = noise(seeds[0], (NZ, NX, NY), 0.05, 0.3984375, ((0, 8),))
    probe = noise(seeds[1], (MODES, 2, WIN, WIN), (WIN * WIN) ** -0.5, 0.046875, (), jnp.float32)
    measured = jnp.clip(jnp.exp(math.log(40.0) - 2.9957323 * jax.random.uniform(seeds[2], (ANGLES, POS, WIN, WIN), jnp.float32) ** block_levels(seeds[2], (ANGLES, POS, WIN, WIN), ((0, 4), (1, 8)), -0.2, 0.2)), 2.0, 40.0)
    angle_index = jax.random.permutation(seeds[3], ANGLES).astype(jnp.int32)
    row_offset = draw_row_offset(jax.random.fold_in(seeds[6], 71), 0)
    col_offset = draw_col_offset(jax.random.fold_in(seeds[6], 71), 0)
    return {"volume": volume, "probe": probe, "measured": measured, "angle_index": angle_index, "row_offset": row_offset, "col_offset": col_offset}


def signed_freq(count):
    index = jnp.arange(count, dtype=jnp.int32)
    return jnp.where(index < count // 2, index, index - count).astype(jnp.float32)

def shear_phases(angle_number):
    theta = math.pi * (angle_number.astype(jnp.float32) + 0.5) / ANGLES - math.pi / 2
    shear_x = -jnp.tan(theta / 2)
    shear_y = jnp.sin(theta)
    cells_y = jnp.arange(NY, dtype=jnp.int32).astype(jnp.float32) - NY / 2
    cells_x = jnp.arange(NX, dtype=jnp.int32).astype(jnp.float32) - NX / 2
    phase_one = -2.0 * math.pi * signed_freq(NX)[:, None] * shear_x * cells_y[None, :] / NX
    phase_two = -2.0 * math.pi * signed_freq(NY)[:, None] * shear_y * cells_x[None, :] / NY
    return (phase_one, phase_two)

def project_block(block, phase_one, phase_two):
    spectrum = jnp.fft.fft(block, axis=1) * jnp.exp(1j * phase_one)[None]
    sheared = jnp.real(jnp.fft.ifft(spectrum, axis=1))
    beam = jnp.fft.fft(sheared, axis=2)
    summed = lax.optimization_barrier(jnp.sum(beam * jnp.exp(1j * phase_two).T[None], axis=1))
    return jnp.real(jnp.fft.ifft(summed, axis=-1))

def backproject_block(grad_rows, phase_one, phase_two):
    cbar = jnp.fft.fft(grad_rows, axis=-1) / NY
    spread = cbar[:, None, :] * jnp.exp(-1j * phase_two).T[None]
    sheared = jnp.real(jnp.fft.ifft(spread, axis=2)) * NY
    spectrum = jnp.fft.fft(sheared, axis=1) / NX * jnp.exp(-1j * phase_one)[None]
    return jnp.real(jnp.fft.ifft(spectrum, axis=1)) * NX

def window_terms(proj_rows, probe_modes, measure, rows_here, cols_here):
    half = WIN // 2
    padded = jnp.pad(proj_rows, ((half, half), (0, 0)))

    def cut_patch(row_start, col_start):
        return lax.dynamic_slice(padded, (row_start + half, col_start), (WIN, WIN))
    patches = jax.vmap(cut_patch)(rows_here, cols_here)
    objects = jnp.exp(1j * patches)
    far = jnp.fft.fft2(probe_modes[None] * objects[:, None])
    intensity = lax.optimization_barrier(jnp.sum(jnp.real(far * jnp.conj(far)), axis=1))
    factor = (1.0 - jnp.sqrt(measure + 1.0) / jnp.sqrt(intensity + 1.0)) / WIN
    back = WIN * WIN * jnp.fft.ifft2(factor[:, None] * far)
    probe_grad = lax.optimization_barrier(jnp.sum(jnp.conj(objects)[:, None] * back, axis=0))
    object_grad = lax.optimization_barrier(jnp.sum(jnp.conj(probe_modes)[None] * back, axis=1))
    patch_grad = jnp.imag(object_grad * jnp.conj(objects))

    def add_patch(index, buffer):
        start_row = rows_here[index] + half
        start_col = cols_here[index]
        current = lax.dynamic_slice(buffer, (start_row, start_col), (WIN, WIN))
        return lax.dynamic_update_slice(buffer, current + patch_grad[index], (start_row, start_col))
    buffer = lax.fori_loop(0, POS, add_patch, jnp.zeros(padded.shape, jnp.float32))
    return (buffer[half:half + NZ], jnp.stack([jnp.real(probe_grad), jnp.imag(probe_grad)], axis=1))

def reference(volume, probe, measured, angle_index, row_offset, col_offset):
    field = volume.astype(jnp.float32)
    block_rows = math.gcd(NZ, 16)
    blocks = field.reshape(NZ // block_rows, block_rows, NX, NY)
    probe_modes = probe[:, 0] + 1j * probe[:, 1]

    def per_angle(carry, inputs):
        volume_acc, probe_acc = carry
        angle_number, measure, rows_here, cols_here = inputs
        phase_one, phase_two = shear_phases(angle_number)

        def forward_block(block):
            return project_block(block, phase_one, phase_two)
        proj_rows = lax.map(forward_block, blocks).reshape(NZ, NY)
        grad_rows, probe_grad = window_terms(proj_rows, probe_modes, measure, rows_here, cols_here)

        def adjoint_block(rows_block):
            return backproject_block(rows_block, phase_one, phase_two)
        grad_blocks = grad_rows.reshape(NZ // block_rows, block_rows, NY)
        field_grad = lax.map(adjoint_block, grad_blocks).reshape(NZ, NX, NY)
        return ((volume_acc + field_grad, probe_acc + probe_grad), None)
    start = (jnp.zeros((NZ, NX, NY), jnp.float32), jnp.zeros((MODES, 2, WIN, WIN), jnp.float32))
    (volume_grad, probe_grad), unused = lax.scan(per_angle, start, (angle_index, measured, row_offset, col_offset))
    return (4.0 * volume_grad, probe_grad / 16.0)
```

```python
import functools
import math

import jax
import jax.numpy as jnp
import numpy as np
from jax import lax
from jax.experimental import pallas as pl
from jax.experimental.pallas import tpu as pltpu
from jax.sharding import PartitionSpec as P

MESH = pl.DeviceIdType.MESH
F32 = jnp.float32
BF16 = jnp.bfloat16
VM = pl.BlockSpec(memory_space=pltpu.VMEM)
SM = pl.BlockSpec(memory_space=pltpu.SMEM)


def split_table(table):
    table = np.asarray(table, np.float32)
    high = table.astype(jnp.bfloat16)
    low = (table - high.astype(np.float32)).astype(jnp.bfloat16)
    return np.stack([high, low])


def split(value):
    high = value.astype(BF16)
    return high, (value - high.astype(F32)).astype(BF16)


def dot(a, b):
    return jnp.dot(a, b, preferred_element_type=F32)


def dot3(a, b):
    return dot(a[0], b[0]) + (dot(a[0], b[1]) + dot(a[1], b[0]))


def packed_forward(n):
    k = np.arange(n // 2)[:, None]
    x = np.arange(n)[None, :]
    turns = 2.0 * np.pi * (k * x % n) / n
    imag = -np.sin(turns)
    imag[0] = np.where(x[0] % 2 == 0, 1.0, -1.0)
    return np.concatenate([np.cos(turns), imag], axis=0)


def wave_tables(n):
    k = np.arange(n // 2)[:, None]
    y = np.arange(n)[None, :]
    turns = 2.0 * np.pi * (k * y % n) / n
    sine = np.sin(turns)
    sine[0] = np.where(y[0] % 2 == 0, 1.0, -1.0)
    return np.stack([np.cos(turns), sine]).astype(np.float32)


def angle_tables(nx, ny, count):
    rot, mix = [], []
    cells_y = np.arange(ny)[None, :] - ny / 2
    cells_x = np.arange(nx)[None, :] - nx / 2
    weight = np.full(nx // 2, 2.0 / nx)
    weight[0] = 1.0 / nx
    for number in range(count):
        theta = math.pi * (number + 0.5) / count - math.pi / 2
        shear_x = -math.tan(theta / 2)
        shear_y = math.sin(theta)
        kx = np.arange(nx // 2)[:, None]
        one = -2.0 * np.pi * kx * shear_x * cells_y / nx
        nyquist_one = 2.0 * np.pi * (nx // 2) * shear_x * cells_y[0] / nx
        sine = np.sin(one)
        sine[0] = np.cos(nyquist_one)
        rot.append(np.stack([np.cos(one), sine]))
        ky = np.arange(ny // 2)[:, None]
        two = -2.0 * np.pi * ky * shear_y * cells_x / ny
        nyquist_two = 2.0 * np.pi * (ny // 2) * shear_y * cells_x[0] / ny
        upper, lower = np.cos(two), np.sin(two)
        lower[0] = np.cos(nyquist_two)
        spectrum = np.fft.rfft(np.concatenate([upper, lower], axis=0), axis=1)
        real = spectrum.real[:, : nx // 2] * weight
        imag = spectrum.imag[:, : nx // 2] * weight
        imag[:, 0] = spectrum.real[:, nx // 2] / nx
        mix.append(np.concatenate([real, imag], axis=1))
    return np.stack(rot).astype(np.float32), np.stack(mix)


def first_row(shape):
    return lax.broadcasted_iota(jnp.int32, shape, 0) == 0


def half_weights(n):
    return jnp.where(first_row((n // 2, 1)), 1.0 / n, 2.0 / n).astype(F32)


def forward_kernel(number, volume, fx, rot, mix, wave, out):
    n = volume.shape[1]
    half = n // 2
    field = volume[0]
    spec = dot(fx[0], field) + dot(fx[1], field)
    real, imag = spec[:half], spec[half:]
    top = first_row((half, 1))
    cosine, raw = rot[0, 0], rot[0, 1]
    sine = jnp.where(top, 0.0, raw)
    turned = jnp.concatenate(
        [real * cosine - imag * sine, real * sine + imag * jnp.where(top, raw, cosine)], axis=0
    )
    beam = dot3((mix[0, 0], mix[1, 0]), split(turned))
    upper, lower = beam[:half], beam[half:]
    cosine, raw = wave[0], wave[1]
    sine = jnp.where(top, 0.0, raw)
    weight = half_weights(wave.shape[2])
    sum_real = weight * jnp.sum(upper * cosine + lower * sine, axis=1, keepdims=True)
    sum_imag = weight * jnp.sum(
        lower * jnp.where(top, raw, cosine) - upper * sine, axis=1, keepdims=True
    )
    out[...] = jnp.sum(
        sum_real * cosine - sum_imag * jnp.where(top, -raw, raw), axis=0, keepdims=True
    )


def exact_dot(a, b):
    return jnp.dot(a, b, precision=lax.Precision.HIGHEST, preferred_element_type=F32)


def window_kernel(
    modes, row_off, col_off, number, row, probe, measured, turn,
    grad_rows, probe_grad,
    gathered, sent, received, angle_sent, angle_rows, mat, wide,
    gs, gr, rs, rr, as_, ar,
):
    depth, angles = gathered.shape[0], angle_rows.shape[0]
    width = row.shape[1]
    window = probe.shape[-1]
    half = window // 2
    g, a = lax.axis_index("gz"), lax.axis_index("angle")

    barrier = pltpu.get_barrier_semaphore()
    for d in range(1, depth):
        pl.semaphore_signal(barrier, inc=1, device_id=(a, lax.rem(g + d, depth)), device_id_type=MESH)
    for d in range(1, angles):
        pl.semaphore_signal(barrier, inc=1, device_id=(lax.rem(a + d, angles), g), device_id_type=MESH)
    pl.semaphore_wait(barrier, depth + angles - 2)

    def push(src, dst, send, recv, device):
        return pltpu.make_async_remote_copy(
            src_ref=src, dst_ref=dst, send_sem=send, recv_sem=recv, device_id=device, device_id_type=MESH
        )

    copies = []
    for d in range(1, depth):
        copies.append(push(row, gathered.at[g], gs.at[d], gr.at[d], (a, lax.rem(g + d, depth))))
        copies[-1].start()
    gathered[g] = row[...]
    for copy in copies:
        copy.wait()

    rows = jnp.concatenate([gathered[z] for z in range(depth)], axis=0)
    row0, col0 = row_off[0, 0], col_off[0, 0]
    iota = lax.broadcasted_iota
    pick = (iota(jnp.int32, (width, window), 0) == iota(jnp.int32, (width, window), 1) + col0).astype(F32)
    pick_t = (iota(jnp.int32, (window, width), 1) == iota(jnp.int32, (window, width), 0) + col0).astype(F32)
    shape = (2 * depth, depth)
    place = (
        iota(jnp.int32, shape, 0) + (half - depth) == iota(jnp.int32, shape, 1) - row0
    ).astype(F32)
    place_t = (
        iota(jnp.int32, shape[::-1], 1) + (half - depth) == iota(jnp.int32, shape[::-1], 0) - row0
    ).astype(F32)
    patch = exact_dot(place, exact_dot(rows, pick))
    obj_real, obj_imag = jnp.cos(patch), jnp.sin(patch)
    low, high = half - depth, half + depth

    for m in range(modes):
        lanes = slice(m * window, (m + 1) * window)
        mat[0:window, lanes] = probe[m, 0]
        mat[window:, lanes] = probe[m, 1]
        mid_real, mid_imag = probe[m, 0, low:high], probe[m, 1, low:high]
        mat[low:high, lanes] = mid_real * obj_real - mid_imag * obj_imag
        mat[window + low : window + high, lanes] = mid_real * obj_imag + mid_imag * obj_real
    left, left_t = (turn[0, 0], turn[0, 1]), (turn[1, 0], turn[1, 1])
    mat[...] = dot3(left, split(mat[...]))
    for m in range(modes):
        lanes = slice(m * window, (m + 1) * window)
        wide[lanes, 0:window] = mat[0:window, lanes]
        wide[lanes, window:] = mat[window:, lanes]
    wide[...] = dot3(split(wide[...]), left_t)
    intensity = jnp.zeros((window, window), F32)
    for m in range(modes):
        lanes = slice(m * window, (m + 1) * window)
        far_real, far_imag = wide[lanes, 0:window], wide[lanes, window:]
        intensity += far_real * far_real + far_imag * far_imag
    factor = (1.0 - jnp.sqrt(measured[0, 0] + 1.0) / jnp.sqrt(intensity + 1.0)) / window
    for m in range(modes):
        lanes = slice(m * window, (m + 1) * window)
        wide[lanes, 0:window] = wide[lanes, 0:window] * factor
        wide[lanes, window:] = wide[lanes, window:] * factor
    wide[...] = dot3(split(wide[...]), left)
    for m in range(modes):
        lanes = slice(m * window, (m + 1) * window)
        mat[0:window, lanes] = wide[lanes, 0:window]
        mat[window:, lanes] = wide[lanes, window:]
    mat[...] = dot3(left_t, split(mat[...]))

    grad_real = jnp.zeros((2 * depth, window), F32)
    grad_imag = jnp.zeros((2 * depth, window), F32)
    for m in range(modes):
        lanes = slice(m * window, (m + 1) * window)
        back_real, back_imag = mat[low:high, lanes], mat[window + low : window + high, lanes]
        mid_real, mid_imag = probe[m, 0, low:high], probe[m, 1, low:high]
        grad_real += mid_real * back_real + mid_imag * back_imag
        grad_imag += mid_real * back_imag - mid_imag * back_real
    patch_grad = grad_imag * obj_real - grad_real * obj_imag
    full = exact_dot(exact_dot(place_t, patch_grad), pick_t)
    for z in range(depth):
        sent[z] = full[z : z + 1]

    copies = []
    for d in range(1, depth):
        peer = lax.rem(g + d, depth)
        copies.append(push(sent.at[peer], received.at[g], rs.at[d], rr.at[d], (a, peer)))
        copies[-1].start()
    received[g] = sent[g]

    for m in range(modes):
        lanes = slice(m * window, (m + 1) * window)
        probe_grad[m, 0] = mat[0:window, lanes] * 0.0625
        probe_grad[m, 1] = mat[window:, lanes] * 0.0625
        back_real, back_imag = mat[low:high, lanes], mat[window + low : window + high, lanes]
        probe_grad[m, 0, low:high] = (obj_real * back_real + obj_imag * back_imag) * 0.0625
        probe_grad[m, 1, low:high] = (obj_real * back_imag - obj_imag * back_real) * 0.0625

    for copy in copies:
        copy.wait()
    total = received[0]
    for z in range(1, depth):
        total = total + received[z]
    angle_sent[:, 0:width] = total
    angle_sent[:, width:] = jnp.zeros((1, 128), F32) + number[0].astype(F32)
    copies = []
    for d in range(1, angles):
        copies.append(push(angle_sent, angle_rows.at[a], as_.at[d], ar.at[d], (lax.rem(a + d, angles), g)))
        copies[-1].start()
    angle_rows[a] = angle_sent[...]
    for copy in copies:
        copy.wait()
    grad_rows[...] = angle_rows[...]


def back_kernel(block, grad_rows, rot, mix_t, wave, fx_t, out, acc):
    step, angles = pl.program_id(0), pl.num_programs(0)
    half, width = wave.shape[1], wave.shape[2]
    row = jnp.zeros((1, width), F32)
    for a in range(grad_rows.shape[0]):
        mine = grad_rows[a, :, width : width + 1] == step.astype(F32)
        row = row + jnp.where(mine, grad_rows[a, :, 0:width], 0.0)
    top = first_row((half, 1))
    cosine, raw = wave[0], wave[1]
    sine = jnp.where(top, 0.0, raw)
    weight = half_weights(width)
    in_real = weight * jnp.sum(row * cosine, axis=1, keepdims=True)
    in_imag = -weight * jnp.sum(row * jnp.where(top, -raw, raw), axis=1, keepdims=True)
    beam = jnp.concatenate(
        [in_real * cosine - in_imag * sine, in_real * sine + in_imag * jnp.where(top, raw, cosine)], axis=0
    )
    turned = dot3((mix_t[0, 0], mix_t[1, 0]), split(beam))
    kx = turned.shape[0] // 2
    real, imag = turned[:kx], turned[kx:]
    top = first_row((kx, 1))
    cosine, raw = rot[0, 0], rot[0, 1]
    sine = jnp.where(top, 0.0, raw)
    back = jnp.concatenate(
        [real * cosine + imag * sine, imag * jnp.where(top, raw, cosine) - real * sine], axis=0
    )

    @pl.when(step == 0)
    def _():
        acc[...] = back

    @pl.when(step > 0)
    def _():
        acc[...] += back

    @pl.when(step == angles - 1)
    def _():
        out[0] = 4.0 * dot3((fx_t[0], fx_t[1]), split(acc[...]))


def local(volume, probe, measured, angle_index, row_offset, col_offset):
    _, nx, ny = volume.shape
    modes, _, window, _ = probe.shape
    depth, angles = lax.axis_size("gz"), lax.axis_size("angle")
    rot, mix = angle_tables(nx, ny, angles)
    mix_pair = split_table(mix)
    mix_t_pair = split_table(np.swapaxes(mix, 1, 2))
    fx = packed_forward(nx)
    fx_pair, fx_t_pair = split_table(fx), split_table(fx.T)
    wave = wave_tables(ny)
    turns = 2.0 * np.pi * (np.arange(window)[:, None] * np.arange(window)[None, :] % window) / window
    cosine, sine = np.cos(turns), np.sin(turns)
    left = np.block([[cosine, sine], [-sine, cosine]])
    turn = np.stack([split_table(left), split_table(left.T)])
    big = 48 * 1024 * 1024

    row = pl.pallas_call(
        forward_kernel,
        grid_spec=pltpu.PrefetchScalarGridSpec(
            num_scalar_prefetch=1,
            grid=(1,),
            in_specs=[
                pl.BlockSpec((1, nx, ny), lambda i, s: (0, 0, 0)),
                pl.BlockSpec((2, nx, nx), lambda i, s: (0, 0, 0)),
                pl.BlockSpec((1, 2, nx // 2, ny), lambda i, s: (s[0], 0, 0, 0)),
                pl.BlockSpec((2, 1, ny, nx), lambda i, s: (0, s[0], 0, 0)),
                pl.BlockSpec((2, ny // 2, ny), lambda i, s: (0, 0, 0)),
            ],
            out_specs=pl.BlockSpec((1, ny), lambda i, s: (0, 0)),
        ),
        out_shape=jax.ShapeDtypeStruct((1, ny), F32),
        compiler_params=pltpu.CompilerParams(vmem_limit_bytes=big),
        name="forward",
    )(angle_index, volume, fx_pair, rot, mix_pair, wave)

    dma = pltpu.SemaphoreType.DMA
    grad_rows, probe_grad = pl.pallas_call(
        functools.partial(window_kernel, modes),
        out_shape=(
            jax.ShapeDtypeStruct((angles, 1, ny + 128), F32),
            jax.ShapeDtypeStruct(probe.shape, F32),
        ),
        in_specs=[SM, SM, SM, VM, VM, VM, VM],
        out_specs=(VM, VM),
        scratch_shapes=[
            pltpu.VMEM((depth, 1, ny), F32),
            pltpu.VMEM((depth, 1, ny), F32),
            pltpu.VMEM((depth, 1, ny), F32),
            pltpu.VMEM((1, ny + 128), F32),
            pltpu.VMEM((angles, 1, ny + 128), F32),
            pltpu.VMEM((2 * window, modes * window), F32),
            pltpu.VMEM((modes * window, 2 * window), F32),
            dma((depth,)), dma((depth,)), dma((depth,)), dma((depth,)), dma((angles,)), dma((angles,)),
        ],
        compiler_params=pltpu.CompilerParams(
            collective_id=0, has_side_effects=True, vmem_limit_bytes=big
        ),
        name="window",
    )(row_offset, col_offset, angle_index, row, probe, measured, turn)

    probe_total = lax.psum(probe_grad, ("angle", "gz"))

    block = jnp.reshape(lax.axis_index("angle"), (1,)).astype(jnp.int32)
    block_rows = nx // angles
    out = pl.pallas_call(
        back_kernel,
        grid_spec=pltpu.PrefetchScalarGridSpec(
            num_scalar_prefetch=1,
            grid=(angles,),
            in_specs=[
                pl.BlockSpec((angles, 1, ny + 128), lambda i, s: (0, 0, 0)),
                pl.BlockSpec((1, 2, nx // 2, ny), lambda i, s: (i, 0, 0, 0)),
                pl.BlockSpec((2, 1, nx, ny), lambda i, s: (0, i, 0, 0)),
                pl.BlockSpec((2, ny // 2, ny), lambda i, s: (0, 0, 0)),
                pl.BlockSpec((2, block_rows, nx), lambda i, s: (0, s[0], 0)),
            ],
            out_specs=pl.BlockSpec((1, block_rows, ny), lambda i, s: (0, 0, 0)),
            scratch_shapes=[pltpu.VMEM((nx, ny), F32)],
        ),
        out_shape=jax.ShapeDtypeStruct((1, block_rows, ny), F32),
        compiler_params=pltpu.CompilerParams(vmem_limit_bytes=big),
        cost_estimate=pl.CostEstimate(flops=4_000_000_000, bytes_accessed=9_000_000, transcendentals=0),
        name="back",
    )(block, grad_rows, rot, mix_t_pair, wave, fx_t_pair)
    return (out, probe_total)


def solution(mesh):
    return jax.shard_map(
        local,
        mesh=mesh,
        in_specs=(
            P("gz", None, None),
            P(),
            P("angle", "gz", None, None),
            P("angle"),
            P("angle", "gz"),
            P("angle", "gz"),
        ),
        out_specs=(P("gz", "angle", None), P()),
        check_vma=False,
    )
```

```python
import functools
import math

import jax
import jax.numpy as jnp
import numpy as np
from jax import lax
from jax.experimental import pallas as pl
from jax.experimental.pallas import tpu as pltpu
from jax.sharding import PartitionSpec as P

MESH = pl.DeviceIdType.MESH
F32 = jnp.float32
BF16 = jnp.bfloat16
VM = pl.BlockSpec(memory_space=pltpu.VMEM)
SM = pl.BlockSpec(memory_space=pltpu.SMEM)


def split_table(table):
    table = np.asarray(table, np.float32)
    high = table.astype(jnp.bfloat16)
    low = (table - high.astype(np.float32)).astype(jnp.bfloat16)
    return np.stack([high, low])


def split(value):
    high = value.astype(BF16)
    return high, (value - high.astype(F32)).astype(BF16)


def dot(a, b):
    return jnp.dot(a, b, preferred_element_type=F32)


def dot3(a, b):
    return dot(a[0], b[0]) + (dot(a[0], b[1]) + dot(a[1], b[0]))


def packed_forward(n):
    k = np.arange(n // 2)[:, None]
    x = np.arange(n)[None, :]
    turns = 2.0 * np.pi * (k * x % n) / n
    imag = -np.sin(turns)
    imag[0] = np.where(x[0] % 2 == 0, 1.0, -1.0)
    return np.concatenate([np.cos(turns), imag], axis=0)


def wave_tables(n):
    k = np.arange(n // 2)[:, None]
    y = np.arange(n)[None, :]
    turns = 2.0 * np.pi * (k * y % n) / n
    sine = np.sin(turns)
    sine[0] = np.where(y[0] % 2 == 0, 1.0, -1.0)
    return np.stack([np.cos(turns), sine]).astype(np.float32)


def angle_tables(nx, ny, count):
    rot, mix = [], []
    cells_y = np.arange(ny)[None, :] - ny / 2
    cells_x = np.arange(nx)[None, :] - nx / 2
    weight = np.full(nx // 2, 2.0 / nx)
    weight[0] = 1.0 / nx
    for number in range(count):
        theta = math.pi * (number + 0.5) / count - math.pi / 2
        shear_x = -math.tan(theta / 2)
        shear_y = math.sin(theta)
        kx = np.arange(nx // 2)[:, None]
        one = -2.0 * np.pi * kx * shear_x * cells_y / nx
        nyquist_one = 2.0 * np.pi * (nx // 2) * shear_x * cells_y[0] / nx
        sine = np.sin(one)
        sine[0] = np.cos(nyquist_one)
        rot.append(np.stack([np.cos(one), sine]))
        ky = np.arange(ny // 2)[:, None]
        two = -2.0 * np.pi * ky * shear_y * cells_x / ny
        nyquist_two = 2.0 * np.pi * (ny // 2) * shear_y * cells_x[0] / ny
        upper, lower = np.cos(two), np.sin(two)
        lower[0] = np.cos(nyquist_two)
        spectrum = np.fft.rfft(np.concatenate([upper, lower], axis=0), axis=1)
        real = spectrum.real[:, : nx // 2] * weight
        imag = spectrum.imag[:, : nx // 2] * weight
        imag[:, 0] = spectrum.real[:, nx // 2] / nx
        mix.append(np.concatenate([real, imag], axis=1))
    return np.stack(rot).astype(np.float32), np.stack(mix)


def first_row(shape):
    return lax.broadcasted_iota(jnp.int32, shape, 0) == 0


def half_weights(n):
    return jnp.where(first_row((n // 2, 1)), 1.0 / n, 2.0 / n).astype(F32)


def forward_kernel(number, volume_hbm, fx_hbm, rot_hbm, mix_hbm, wave_hbm, out, volume, fx, rot, mix, wave, sems):
    angle = number[0]
    loads = [
        pltpu.make_async_copy(volume_hbm, volume, sems.at[0]),
        pltpu.make_async_copy(fx_hbm, fx, sems.at[1]),
        pltpu.make_async_copy(rot_hbm.at[pl.ds(angle, 1)], rot, sems.at[2]),
        pltpu.make_async_copy(mix_hbm.at[:, pl.ds(angle, 1)], mix, sems.at[3]),
        pltpu.make_async_copy(wave_hbm, wave, sems.at[4]),
    ]
    for load in loads:
        load.start()
    n = volume.shape[1]
    half = n // 2
    loads[0].wait()
    loads[1].wait()
    field = volume[0]
    spec = dot(fx[0], field) + dot(fx[1], field)
    real, imag = spec[:half], spec[half:]
    loads[2].wait()
    top = first_row((half, 1))
    cosine, raw = rot[0, 0], rot[0, 1]
    sine = jnp.where(top, 0.0, raw)
    turned = jnp.concatenate(
        [real * cosine - imag * sine, real * sine + imag * jnp.where(top, raw, cosine)], axis=0
    )
    loads[3].wait()
    beam = dot3((mix[0, 0], mix[1, 0]), split(turned))
    loads[4].wait()
    upper, lower = beam[:half], beam[half:]
    cosine, raw = wave[0], wave[1]
    sine = jnp.where(top, 0.0, raw)
    weight = half_weights(wave.shape[2])
    sum_real = weight * jnp.sum(upper * cosine + lower * sine, axis=1, keepdims=True)
    sum_imag = weight * jnp.sum(
        lower * jnp.where(top, raw, cosine) - upper * sine, axis=1, keepdims=True
    )
    out[...] = jnp.sum(
        sum_real * cosine - sum_imag * jnp.where(top, -raw, raw), axis=0, keepdims=True
    )


def exact_dot(a, b):
    return jnp.dot(a, b, precision=lax.Precision.HIGHEST, preferred_element_type=F32)


def reduce_plan(angles, depth, tiles):
    angle_bits = [("angle", b) for b in range(angles.bit_length() - 1)]
    gz_bits = [("gz", b) for b in range(1, depth.bit_length() - 1)]
    first = [("gz", 0)] + angle_bits + gz_bits
    second = [("gz", 0)] + angle_bits[::-1] + gz_bits[::-1]
    if tiles % (2 * angles * depth) == 0:
        return [first, second]
    return [first]


class Reducer:
    def __init__(self, place, plan, acc, land, total, sems):
        self.place, self.plan, self.acc, self.land, self.total = place, plan, acc, land, total
        self.sems = sems
        count = len(plan)
        self.length = [acc.shape[0] // count] * count
        self.start = [i * self.length[0] for i in range(count)]
        self.offset = [i * self.length[0] for i in range(count)]
        self.stages = len(plan[0])
        self.flying = []

    def partner(self, axis, bit):
        index = self.place[axis]
        mine = lax.rem(index // (1 << bit), 2)
        other = dict(self.place)
        other[axis] = index + (1 - 2 * mine) * (1 << bit)
        return mine, (other["angle"], other["gz"])

    def copy(self, src, dst, stage, stream, device):
        send, recv = self.sems
        made = pltpu.make_async_remote_copy(
            src_ref=src, dst_ref=dst, send_sem=send.at[stage, stream], recv_sem=recv.at[stage, stream],
            device_id=device, device_id_type=MESH,
        )
        made.start()
        return made

    def start_halving(self, stage, i):
        mine, device = self.partner(*self.plan[i][stage])
        size = self.length[i] // 2
        keep = self.start[i] + mine * size
        other = self.start[i] + (1 - mine) * size
        landing = pl.ds(self.offset[i], size)
        made = self.copy(self.acc.at[pl.ds(other, size)], self.land.at[landing], stage, i, device)
        self.flying.append((made, keep, size, landing))

    def start_doubling(self, stage, i):
        mine, device = self.partner(*self.plan[i][2 * self.stages - 1 - stage])
        rows = self.total.at[pl.ds(self.start[i], self.length[i])]
        made = self.copy(rows, rows, stage, i, device)
        self.start[i] = self.start[i] - mine * self.length[i]
        self.length[i] *= 2
        self.flying.append((made,))

    def begin(self):
        self.stage = 0
        for i in range(len(self.plan)):
            self.start_halving(0, i)

    def advance(self):
        flying, self.flying = self.flying, []
        after = self.stage + 1
        for i, (made, *rest) in enumerate(flying):
            made.wait()
            if self.stage < self.stages:
                keep, size, landing = rest
                rows = pl.ds(keep, size)
                into = self.acc if after < self.stages else self.total
                into[rows] = self.acc[rows] + self.land[landing]
                self.start[i], self.length[i] = keep, size
                self.offset[i] += size
            if after < self.stages:
                self.start_halving(after, i)
            elif after < 2 * self.stages:
                self.start_doubling(after, i)
        self.stage = after


def back_columns(j, angle_rows, wave, weights):
    half, width = wave.shape[1], wave.shape[2]
    row = jnp.zeros((1, width), F32)
    for a in range(angle_rows.shape[0]):
        mine = angle_rows[a, :, width : width + 1] == float(j)
        row = row + jnp.where(mine, angle_rows[a, :, 0:width], 0.0)
    cosine, raw = wave[0], wave[1]
    top = first_row((half, 1))
    weight = half_weights(width)
    weights[j, 0] = weight * jnp.sum(row * cosine, axis=1, keepdims=True)
    weights[j, 1] = -weight * jnp.sum(row * jnp.where(top, -raw, raw), axis=1, keepdims=True)


def back_part(j, cols, weights, rot, mix_t, wave, acc):
    in_real, in_imag = weights[j, 0], weights[j, 1]
    cosine, raw = wave[0, :, cols], wave[1, :, cols]
    top = first_row((cosine.shape[0], 1))
    sine = jnp.where(top, 0.0, raw)
    beam = jnp.concatenate(
        [in_real * cosine - in_imag * sine, in_real * sine + in_imag * jnp.where(top, raw, cosine)], axis=0
    )
    turned = dot3((mix_t[0, j], mix_t[1, j]), split(beam))
    kx = turned.shape[0] // 2
    real, imag = turned[:kx], turned[kx:]
    top = first_row((kx, 1))
    cosine, raw = rot[j, 0, :, cols], rot[j, 1, :, cols]
    sine = jnp.where(top, 0.0, raw)
    upper = real * cosine + imag * sine
    lower = imag * jnp.where(top, raw, cosine) - real * sine
    if j > 0:
        upper, lower = acc[:kx, cols] + upper, acc[kx:, cols] + lower
    acc[:kx, cols] = upper
    acc[kx:, cols] = lower


def window_kernel(
    modes, plan, row_off, col_off, number, row, probe_hbm, measured_hbm, turn_hbm, wave_hbm, rot_hbm, mix_hbm, fx_hbm,
    out, probe_out,
    gathered, sent, received, angle_sent, angle_rows, mat, wide, probe, measured, turn, base, thin, weights,
    wave, rot, mix_t, fx_t, field, acc, land, summed,
    gs, gr, rs, rr, as_, ar, tables, reduce_send, reduce_recv,
):
    depth, angles = gathered.shape[0], angle_rows.shape[0]
    width = row.shape[1]
    window = probe.shape[-1]
    half = window // 2
    g, a = lax.axis_index("gz"), lax.axis_index("angle")

    block_rows = fx_t.shape[1]
    early = [
        pltpu.make_async_copy(turn_hbm, turn, tables.at[4]),
        pltpu.make_async_copy(probe_hbm, probe, tables.at[5]),
        pltpu.make_async_copy(measured_hbm, measured, tables.at[6]),
    ]
    for load in early:
        load.start()
    loads = [
        pltpu.make_async_copy(wave_hbm, wave, tables.at[0]),
        pltpu.make_async_copy(rot_hbm, rot, tables.at[1]),
        pltpu.make_async_copy(mix_hbm, mix_t, tables.at[2]),
        pltpu.make_async_copy(fx_hbm.at[:, pl.ds(a * block_rows, block_rows)], fx_t, tables.at[3]),
    ]
    barrier = pltpu.get_barrier_semaphore()
    for d in range(1, depth):
        pl.semaphore_signal(barrier, inc=1, device_id=(a, lax.rem(g + d, depth)), device_id_type=MESH)
    for d in range(1, angles):
        pl.semaphore_signal(barrier, inc=1, device_id=(lax.rem(a + d, angles), g), device_id_type=MESH)
    pl.semaphore_wait(barrier, depth + angles - 2)

    def push(src, dst, send, recv, device):
        return pltpu.make_async_remote_copy(
            src_ref=src, dst_ref=dst, send_sem=send, recv_sem=recv, device_id=device, device_id_type=MESH
        )

    copies = []
    for d in range(1, depth):
        copies.append(push(row, gathered.at[g], gs.at[d], gr.at[d], (a, lax.rem(g + d, depth))))
        copies[-1].start()
    gathered[g] = row[...]
    for load in early:
        load.wait()
    for load in loads:
        load.start()

    row0, col0 = row_off[0, 0], col_off[0, 0]
    iota = lax.broadcasted_iota
    pick = (iota(jnp.int32, (width, window), 0) == iota(jnp.int32, (width, window), 1) + col0).astype(F32)
    pick_t = (iota(jnp.int32, (window, width), 1) == iota(jnp.int32, (window, width), 0) + col0).astype(F32)
    shape = (2 * depth, depth)
    place = (
        iota(jnp.int32, shape, 0) + (half - depth) == iota(jnp.int32, shape, 1) - row0
    ).astype(F32)
    place_t = (
        iota(jnp.int32, shape[::-1], 1) + (half - depth) == iota(jnp.int32, shape[::-1], 0) - row0
    ).astype(F32)
    low, high, band = half - depth, half + depth, 2 * depth
    left, left_t = (turn[0, 0], turn[0, 1]), (turn[1, 0], turn[1, 1])

    def lanes(m):
        return slice(m * window, (m + 1) * window)

    for m in range(modes):
        wide[lanes(m), 0:window] = probe[m, 0]
        wide[lanes(m), window:] = probe[m, 1]
    wide[...] = dot3(split(wide[...]), left_t)
    for m in range(modes):
        mat[0:window, lanes(m)] = wide[lanes(m), 0:window]
        mat[window:, lanes(m)] = wide[lanes(m), window:]
    base[...] = dot3(left, split(mat[...]))
    for copy in copies:
        copy.wait()

    rows = jnp.concatenate([gathered[z] for z in range(depth)], axis=0)
    patch = exact_dot(place, exact_dot(rows, pick))
    obj_real, obj_imag = jnp.cos(patch), jnp.sin(patch)
    for m in range(modes):
        mid_real, mid_imag = probe[m, 0, low:high], probe[m, 1, low:high]
        thin[m * band : (m + 1) * band, 0:window] = mid_real * obj_real - mid_imag * obj_imag - mid_real
        thin[m * band : (m + 1) * band, window:] = mid_real * obj_imag + mid_imag * obj_real - mid_imag
    change = dot3(split(thin[...]), left_t)
    change = jnp.concatenate(
        [
            jnp.concatenate([change[m * band : (m + 1) * band, c : c + window] for m in range(modes)], axis=1)
            for c in (0, window)
        ],
        axis=0,
    )
    near = tuple(
        jnp.concatenate([part[:, low:high], part[:, window + low : window + high]], axis=1) for part in left
    )
    mat[...] = base[...] + dot3(near, split(change))
    intensity = jnp.zeros((window, window), F32)
    for m in range(modes):
        far_real, far_imag = mat[0:window, lanes(m)], mat[window:, lanes(m)]
        intensity += far_real * far_real + far_imag * far_imag
    factor = (1.0 - jnp.sqrt(measured[0, 0] + 1.0) / jnp.sqrt(intensity + 1.0)) / window
    for m in range(modes):
        mat[0:window, lanes(m)] = mat[0:window, lanes(m)] * factor
        mat[window:, lanes(m)] = mat[window:, lanes(m)] * factor
    mat[...] = dot3(left_t, split(mat[...]))
    for m in range(modes):
        wide[lanes(m), 0:window] = mat[0:window, lanes(m)]
        wide[lanes(m), window:] = mat[window:, lanes(m)]
    wide[...] = dot3(split(wide[...]), left)

    tiles = window // 8
    shape = (tiles, 8, window)
    part = (depth // 4, 8, window)
    grad_real = jnp.zeros((band, window), F32)
    grad_imag = jnp.zeros((band, window), F32)
    for m in range(modes):
        first = m * window
        at = 2 * m * tiles
        acc[at : at + tiles] = wide[lanes(m), 0:window].reshape(shape) * 0.0625
        acc[at + tiles : at + 2 * tiles] = wide[lanes(m), window:].reshape(shape) * 0.0625
        middle = slice(first + low, first + high)
        back_real, back_imag = wide[middle, 0:window], wide[middle, window:]
        top_tile, end_tile = at + low // 8, at + high // 8
        acc[top_tile:end_tile] = (obj_real * back_real + obj_imag * back_imag).reshape(part) * 0.0625
        acc[top_tile + tiles : end_tile + tiles] = (
            obj_real * back_imag - obj_imag * back_real
        ).reshape(part) * 0.0625
    reducer = Reducer({"angle": a, "gz": g}, plan, acc, land, summed, (reduce_send, reduce_recv))
    reducer.begin()

    for m in range(modes):
        middle = slice(m * window + low, m * window + high)
        back_real, back_imag = wide[middle, 0:window], wide[middle, window:]
        mid_real, mid_imag = probe[m, 0, low:high], probe[m, 1, low:high]
        grad_real += mid_real * back_real + mid_imag * back_imag
        grad_imag += mid_real * back_imag - mid_imag * back_real
    patch_grad = grad_imag * obj_real - grad_real * obj_imag
    full = exact_dot(exact_dot(place_t, patch_grad), pick_t)
    for z in range(depth):
        sent[z] = full[z : z + 1]
    copies = []
    for d in range(1, depth):
        peer = lax.rem(g + d, depth)
        copies.append(push(sent.at[peer], received.at[g], rs.at[d], rr.at[d], (a, peer)))
        copies[-1].start()
    received[g] = sent[g]
    reducer.advance()
    for copy in copies:
        copy.wait()
    total = received[0]
    for z in range(1, depth):
        total = total + received[z]
    angle_sent[:, 0:width] = total
    angle_sent[:, width:] = jnp.zeros((1, 128), F32) + number[0].astype(F32)
    copies = []
    for d in range(1, angles):
        copies.append(push(angle_sent, angle_rows.at[a], as_.at[d], ar.at[d], (lax.rem(a + d, angles), g)))
        copies[-1].start()
    angle_rows[a] = angle_sent[...]
    for copy in copies:
        copy.wait()
    for load in loads:
        load.wait()

    block = width // 2
    work = []
    for c in range(2):
        cols = slice(c * block, (c + 1) * block)
        for j in range(angles):
            if c == 0:
                work.append(functools.partial(back_columns, j, angle_rows, wave, weights))
            work.append(functools.partial(back_part, j, cols, weights, rot, mix_t, wave, field))

        def finish(cols):
            out[0, :, cols] = 4.0 * dot3((fx_t[0], fx_t[1]), split(field[:, cols]))

        work.append(functools.partial(finish, cols))
    steps = 2 * reducer.stages - 1
    done = 0
    for step in range(steps):
        until = min(len(work), -(-len(work) * (step + 1) // (steps - 1)))
        for task in work[done:until]:
            task()
        done = until
        reducer.advance()
    probe_out[...] = summed[...]


def local(volume, probe, measured, angle_index, row_offset, col_offset):
    _, nx, ny = volume.shape
    modes, _, window, _ = probe.shape
    depth, angles = lax.axis_size("gz"), lax.axis_size("angle")
    rot, mix = angle_tables(nx, ny, angles)
    mix_pair = split_table(mix)
    mix_t_pair = split_table(np.swapaxes(mix, 1, 2))
    fx = packed_forward(nx)
    fx_pair, fx_t_pair = split_table(fx), split_table(fx.T)
    wave = wave_tables(ny)
    turns = 2.0 * np.pi * (np.arange(window)[:, None] * np.arange(window)[None, :] % window) / window
    cosine, sine = np.cos(turns), np.sin(turns)
    left = np.block([[cosine, sine], [-sine, cosine]])
    turn = np.stack([split_table(left), split_table(left.T)])
    big = 60 * 1024 * 1024
    hbm = pl.BlockSpec(memory_space=pl.ANY)

    row = pl.pallas_call(
        forward_kernel,
        in_specs=[SM] + [hbm] * 5,
        out_specs=VM,
        scratch_shapes=[
            pltpu.VMEM((1, nx, ny), BF16),
            pltpu.VMEM(fx_pair.shape, BF16),
            pltpu.VMEM((1, 2, nx // 2, ny), F32),
            pltpu.VMEM((2, 1, ny, nx), BF16),
            pltpu.VMEM(wave.shape, F32),
            pltpu.SemaphoreType.DMA((5,)),
        ],
        out_shape=jax.ShapeDtypeStruct((1, ny), F32),
        compiler_params=pltpu.CompilerParams(vmem_limit_bytes=big),
        name="forward",
    )(angle_index, volume, fx_pair, rot, mix_pair, wave)

    dma = pltpu.SemaphoreType.DMA
    block_rows = nx // angles
    tiles = modes * 2 * window // 8
    plan = reduce_plan(angles, depth, tiles)
    stages = 2 * len(plan[0])
    out, probe_total = pl.pallas_call(
        functools.partial(window_kernel, modes, plan),
        out_shape=(
            jax.ShapeDtypeStruct((1, block_rows, ny), F32),
            jax.ShapeDtypeStruct((tiles, 8, window), F32),
        ),
        in_specs=[SM, SM, SM, VM] + [hbm] * 7,
        out_specs=(VM, VM),
        scratch_shapes=[
            pltpu.VMEM((depth, 1, ny), F32),
            pltpu.VMEM((depth, 1, ny), F32),
            pltpu.VMEM((depth, 1, ny), F32),
            pltpu.VMEM((1, ny + 128), F32),
            pltpu.VMEM((angles, 1, ny + 128), F32),
            pltpu.VMEM((2 * window, modes * window), F32),
            pltpu.VMEM((modes * window, 2 * window), F32),
            pltpu.VMEM(probe.shape, F32),
            pltpu.VMEM(measured.shape, F32),
            pltpu.VMEM(turn.shape, BF16),
            pltpu.VMEM((2 * window, modes * window), F32),
            pltpu.VMEM((modes * 2 * depth, 2 * window), F32),
            pltpu.VMEM((angles, 2, ny // 2, 1), F32),
            pltpu.VMEM(wave.shape, F32),
            pltpu.VMEM(rot.shape, F32),
            pltpu.VMEM(mix_t_pair.shape, BF16),
            pltpu.VMEM((2, block_rows, nx), BF16),
            pltpu.VMEM((nx, ny), F32),
            pltpu.VMEM((tiles, 8, window), F32),
            pltpu.VMEM((tiles, 8, window), F32),
            pltpu.VMEM((tiles, 8, window), F32),
            dma((depth,)), dma((depth,)), dma((depth,)), dma((depth,)), dma((angles,)), dma((angles,)),
            dma((7,)), dma((stages, len(plan))), dma((stages, len(plan))),
        ],
        compiler_params=pltpu.CompilerParams(
            collective_id=0, has_side_effects=True, vmem_limit_bytes=big
        ),
        name="window",
    )(row_offset, col_offset, angle_index, row, probe, measured, turn, wave, rot, mix_t_pair, fx_t_pair)
    return (out, probe_total.reshape(probe.shape))


def solution(mesh):
    return jax.shard_map(
        local,
        mesh=mesh,
        in_specs=(
            P("gz", None, None),
            P(),
            P("angle", "gz", None, None),
            P("angle"),
            P("angle", "gz"),
            P("angle", "gz"),
        ),
        out_specs=(P("gz", "angle", None), P()),
        check_vma=False,
    )
```

```python
import functools
import math

import jax
import jax.numpy as jnp
import numpy as np
from jax import lax
from jax.experimental import pallas as pl
from jax.experimental.pallas import tpu as pltpu
from jax.sharding import PartitionSpec as P

MESH = pl.DeviceIdType.MESH
F32 = jnp.float32
BF16 = jnp.bfloat16
VM = pl.BlockSpec(memory_space=pltpu.VMEM)
SM = pl.BlockSpec(memory_space=pltpu.SMEM)


def split_table(table):
    table = np.asarray(table, np.float32)
    high = table.astype(jnp.bfloat16)
    low = (table - high.astype(np.float32)).astype(jnp.bfloat16)
    return np.stack([high, low])


def split(value):
    high = value.astype(BF16)
    return high, (value - high.astype(F32)).astype(BF16)


def dot(a, b):
    return jnp.dot(a, b, preferred_element_type=F32)


def dot3(a, b):
    return dot(a[0], b[0]) + (dot(a[0], b[1]) + dot(a[1], b[0]))


def packed_forward(n):
    k = np.arange(n // 2)[:, None]
    x = np.arange(n)[None, :]
    turns = 2.0 * np.pi * (k * x % n) / n
    imag = -np.sin(turns)
    imag[0] = np.where(x[0] % 2 == 0, 1.0, -1.0)
    return np.concatenate([np.cos(turns), imag], axis=0)


def wave_tables(n):
    k = np.arange(n // 2)[:, None]
    y = np.arange(n)[None, :]
    turns = 2.0 * np.pi * (k * y % n) / n
    sine = np.sin(turns)
    sine[0] = np.where(y[0] % 2 == 0, 1.0, -1.0)
    return np.stack([np.cos(turns), sine]).astype(np.float32)


def angle_tables(nx, ny, count):
    rot, mix = [], []
    cells_y = np.arange(ny)[None, :] - ny / 2
    cells_x = np.arange(nx)[None, :] - nx / 2
    weight = np.full(nx // 2, 2.0 / nx)
    weight[0] = 1.0 / nx
    for number in range(count):
        theta = math.pi * (number + 0.5) / count - math.pi / 2
        shear_x = -math.tan(theta / 2)
        shear_y = math.sin(theta)
        kx = np.arange(nx // 2)[:, None]
        one = -2.0 * np.pi * kx * shear_x * cells_y / nx
        nyquist_one = 2.0 * np.pi * (nx // 2) * shear_x * cells_y[0] / nx
        sine = np.sin(one)
        sine[0] = np.cos(nyquist_one)
        rot.append(np.stack([np.cos(one), sine]))
        ky = np.arange(ny // 2)[:, None]
        two = -2.0 * np.pi * ky * shear_y * cells_x / ny
        nyquist_two = 2.0 * np.pi * (ny // 2) * shear_y * cells_x[0] / ny
        upper, lower = np.cos(two), np.sin(two)
        lower[0] = np.cos(nyquist_two)
        spectrum = np.fft.rfft(np.concatenate([upper, lower], axis=0), axis=1)
        real = spectrum.real[:, : nx // 2] * weight
        imag = spectrum.imag[:, : nx // 2] * weight
        imag[:, 0] = spectrum.real[:, nx // 2] / nx
        mix.append(np.concatenate([real, imag], axis=1))
    return np.stack(rot).astype(np.float32), np.stack(mix)


def first_row(shape):
    return lax.broadcasted_iota(jnp.int32, shape, 0) == 0


def half_weights(n):
    return jnp.where(first_row((n // 2, 1)), 1.0 / n, 2.0 / n).astype(F32)


def forward_kernel(number, volume_hbm, fx_hbm, rot_hbm, mix_hbm, wave_hbm, out, volume, fx, rot, mix, wave, sems):
    angle = number[0]
    loads = [
        pltpu.make_async_copy(volume_hbm, volume, sems.at[0]),
        pltpu.make_async_copy(fx_hbm, fx, sems.at[1]),
        pltpu.make_async_copy(rot_hbm.at[pl.ds(angle, 1)], rot, sems.at[2]),
        pltpu.make_async_copy(mix_hbm.at[:, pl.ds(angle, 1)], mix, sems.at[3]),
        pltpu.make_async_copy(wave_hbm, wave, sems.at[4]),
    ]
    for load in loads:
        load.start()
    n = volume.shape[1]
    half = n // 2
    loads[0].wait()
    loads[1].wait()
    field = volume[0]
    spec = dot(fx[0], field) + dot(fx[1], field)
    real, imag = spec[:half], spec[half:]
    loads[2].wait()
    top = first_row((half, 1))
    cosine, raw = rot[0, 0], rot[0, 1]
    sine = jnp.where(top, 0.0, raw)
    turned = jnp.concatenate(
        [real * cosine - imag * sine, real * sine + imag * jnp.where(top, raw, cosine)], axis=0
    )
    loads[3].wait()
    beam = dot3((mix[0, 0], mix[1, 0]), split(turned))
    loads[4].wait()
    upper, lower = beam[:half], beam[half:]
    cosine, raw = wave[0], wave[1]
    sine = jnp.where(top, 0.0, raw)
    weight = half_weights(wave.shape[2])
    sum_real = weight * jnp.sum(upper * cosine + lower * sine, axis=1, keepdims=True)
    sum_imag = weight * jnp.sum(
        lower * jnp.where(top, raw, cosine) - upper * sine, axis=1, keepdims=True
    )
    out[...] = jnp.sum(
        sum_real * cosine - sum_imag * jnp.where(top, -raw, raw), axis=0, keepdims=True
    )


def exact_dot(a, b):
    return jnp.dot(a, b, precision=lax.Precision.HIGHEST, preferred_element_type=F32)


def reduce_plan(angles, depth, tiles):
    angle_bits = [("angle", b) for b in range(angles.bit_length() - 1)]
    gz_bits = [("gz", b) for b in range(1, depth.bit_length() - 1)]
    core = [("gz", 0)]
    along_x = core + angle_bits + gz_bits
    along_y = core + angle_bits[::-1] + gz_bits
    z_then_x = core + gz_bits + angle_bits
    z_then_y = core + gz_bits + angle_bits[::-1]
    unit = angles * depth
    if tiles != 8 * unit:
        return [(along_x, tiles)]
    return [
        (along_x, 2 * unit), (along_y, 2 * unit), (z_then_x, unit),
        (z_then_y, unit), (along_x, unit), (along_y, unit),
    ]


class Reducer:
    def __init__(self, place, plan, acc, land, total, sems):
        self.place, self.acc, self.land, self.total = place, acc, land, total
        self.sems = sems
        self.plan = [order for order, _ in plan]
        self.length = [size for _, size in plan]
        self.start = [sum(self.length[:i]) for i in range(len(plan))]
        self.offset = list(self.start)
        self.stages = len(self.plan[0])
        self.flying = []

    def partner(self, axis, bit):
        index = self.place[axis]
        mine = lax.rem(index // (1 << bit), 2)
        other = dict(self.place)
        other[axis] = index + (1 - 2 * mine) * (1 << bit)
        return mine, (other["angle"], other["gz"])

    def copy(self, src, dst, stage, stream, device):
        send, recv = self.sems
        made = pltpu.make_async_remote_copy(
            src_ref=src, dst_ref=dst, send_sem=send.at[stage, stream], recv_sem=recv.at[stage, stream],
            device_id=device, device_id_type=MESH,
        )
        made.start()
        return made

    def start_halving(self, stage, i):
        mine, device = self.partner(*self.plan[i][stage])
        size = self.length[i] // 2
        keep = self.start[i] + mine * size
        other = self.start[i] + (1 - mine) * size
        landing = pl.ds(self.offset[i], size)
        made = self.copy(self.acc.at[pl.ds(other, size)], self.land.at[landing], stage, i, device)
        self.flying.append((made, keep, size, landing))

    def start_doubling(self, stage, i):
        mine, device = self.partner(*self.plan[i][2 * self.stages - 1 - stage])
        rows = self.total.at[pl.ds(self.start[i], self.length[i])]
        made = self.copy(rows, rows, stage, i, device)
        self.start[i] = self.start[i] - mine * self.length[i]
        self.length[i] *= 2
        self.flying.append((made,))

    def begin(self):
        self.stage = 0
        for i in range(len(self.plan)):
            self.start_halving(0, i)

    def advance(self):
        flying, self.flying = self.flying, []
        after = self.stage + 1
        for i, (made, *rest) in enumerate(flying):
            made.wait()
            if self.stage < self.stages:
                keep, size, landing = rest
                rows = pl.ds(keep, size)
                into = self.acc if after < self.stages else self.total
                into[rows] = self.acc[rows] + self.land[landing]
                self.start[i], self.length[i] = keep, size
                self.offset[i] += size
            if after < self.stages:
                self.start_halving(after, i)
            elif after < 2 * self.stages:
                self.start_doubling(after, i)
        self.stage = after


def back_columns(j, angle_rows, wave, weights):
    half, width = wave.shape[1], wave.shape[2]
    row = jnp.zeros((1, width), F32)
    for a in range(angle_rows.shape[0]):
        mine = angle_rows[a, :, width : width + 1] == float(j)
        row = row + jnp.where(mine, angle_rows[a, :, 0:width], 0.0)
    cosine, raw = wave[0], wave[1]
    top = first_row((half, 1))
    weight = half_weights(width)
    weights[j, 0] = weight * jnp.sum(row * cosine, axis=1, keepdims=True)
    weights[j, 1] = -weight * jnp.sum(row * jnp.where(top, -raw, raw), axis=1, keepdims=True)


def back_part(j, cols, weights, rot, mix_t, wave, acc):
    in_real, in_imag = weights[j, 0], weights[j, 1]
    cosine, raw = wave[0, :, cols], wave[1, :, cols]
    top = first_row((cosine.shape[0], 1))
    sine = jnp.where(top, 0.0, raw)
    beam = jnp.concatenate(
        [in_real * cosine - in_imag * sine, in_real * sine + in_imag * jnp.where(top, raw, cosine)], axis=0
    )
    turned = dot3((mix_t[0, j], mix_t[1, j]), split(beam))
    kx = turned.shape[0] // 2
    real, imag = turned[:kx], turned[kx:]
    top = first_row((kx, 1))
    cosine, raw = rot[j, 0, :, cols], rot[j, 1, :, cols]
    sine = jnp.where(top, 0.0, raw)
    upper = real * cosine + imag * sine
    lower = imag * jnp.where(top, raw, cosine) - real * sine
    if j > 0:
        upper, lower = acc[:kx, cols] + upper, acc[kx:, cols] + lower
    acc[:kx, cols] = upper
    acc[kx:, cols] = lower


def window_kernel(
    modes, plan, row_off, col_off, number, row, probe_hbm, measured_hbm, turn_hbm, wave_hbm, rot_hbm, mix_hbm, fx_hbm,
    out, probe_out,
    gathered, sent, received, angle_sent, angle_rows, mat, wide, probe, measured, turn, base, thin, weights,
    wave, rot, mix_t, fx_t, field, acc, land, summed,
    gs, gr, rs, rr, as_, ar, tables, reduce_send, reduce_recv,
):
    depth, angles = gathered.shape[0], angle_rows.shape[0]
    width = row.shape[1]
    window = probe.shape[-1]
    half = window // 2
    g, a = lax.axis_index("gz"), lax.axis_index("angle")

    block_rows = fx_t.shape[1]
    early = [
        pltpu.make_async_copy(turn_hbm, turn, tables.at[4]),
        pltpu.make_async_copy(probe_hbm, probe, tables.at[5]),
        pltpu.make_async_copy(measured_hbm, measured, tables.at[6]),
    ]
    for load in early:
        load.start()
    loads = [
        pltpu.make_async_copy(wave_hbm, wave, tables.at[0]),
        pltpu.make_async_copy(rot_hbm, rot, tables.at[1]),
        pltpu.make_async_copy(mix_hbm, mix_t, tables.at[2]),
        pltpu.make_async_copy(fx_hbm.at[:, pl.ds(a * block_rows, block_rows)], fx_t, tables.at[3]),
    ]
    barrier = pltpu.get_barrier_semaphore()
    for d in range(1, depth):
        pl.semaphore_signal(barrier, inc=1, device_id=(a, lax.rem(g + d, depth)), device_id_type=MESH)
    for d in range(1, angles):
        pl.semaphore_signal(barrier, inc=1, device_id=(lax.rem(a + d, angles), g), device_id_type=MESH)
    pl.semaphore_wait(barrier, depth + angles - 2)

    def push(src, dst, send, recv, device):
        return pltpu.make_async_remote_copy(
            src_ref=src, dst_ref=dst, send_sem=send, recv_sem=recv, device_id=device, device_id_type=MESH
        )

    copies = []
    for d in range(1, depth):
        copies.append(push(row, gathered.at[g], gs.at[d], gr.at[d], (a, lax.rem(g + d, depth))))
        copies[-1].start()
    gathered[g] = row[...]
    for load in early:
        load.wait()
    for load in loads:
        load.start()

    row0, col0 = row_off[0, 0], col_off[0, 0]
    iota = lax.broadcasted_iota
    pick = (iota(jnp.int32, (width, window), 0) == iota(jnp.int32, (width, window), 1) + col0).astype(F32)
    pick_t = (iota(jnp.int32, (window, width), 1) == iota(jnp.int32, (window, width), 0) + col0).astype(F32)
    shape = (2 * depth, depth)
    place = (
        iota(jnp.int32, shape, 0) + (half - depth) == iota(jnp.int32, shape, 1) - row0
    ).astype(F32)
    place_t = (
        iota(jnp.int32, shape[::-1], 1) + (half - depth) == iota(jnp.int32, shape[::-1], 0) - row0
    ).astype(F32)
    low, high, band = half - depth, half + depth, 2 * depth
    left, left_t = (turn[0, 0], turn[0, 1]), (turn[1, 0], turn[1, 1])

    def lanes(m):
        return slice(m * window, (m + 1) * window)

    for m in range(modes):
        wide[lanes(m), 0:window] = probe[m, 0]
        wide[lanes(m), window:] = probe[m, 1]
    wide[...] = dot3(split(wide[...]), left_t)
    for m in range(modes):
        mat[0:window, lanes(m)] = wide[lanes(m), 0:window]
        mat[window:, lanes(m)] = wide[lanes(m), window:]
    base[...] = dot3(left, split(mat[...]))
    for copy in copies:
        copy.wait()

    rows = jnp.concatenate([gathered[z] for z in range(depth)], axis=0)
    patch = exact_dot(place, exact_dot(rows, pick))
    obj_real, obj_imag = jnp.cos(patch), jnp.sin(patch)
    for m in range(modes):
        mid_real, mid_imag = probe[m, 0, low:high], probe[m, 1, low:high]
        thin[m * band : (m + 1) * band, 0:window] = mid_real * obj_real - mid_imag * obj_imag - mid_real
        thin[m * band : (m + 1) * band, window:] = mid_real * obj_imag + mid_imag * obj_real - mid_imag
    change = dot3(split(thin[...]), left_t)
    change = jnp.concatenate(
        [
            jnp.concatenate([change[m * band : (m + 1) * band, c : c + window] for m in range(modes)], axis=1)
            for c in (0, window)
        ],
        axis=0,
    )
    near = tuple(
        jnp.concatenate([part[:, low:high], part[:, window + low : window + high]], axis=1) for part in left
    )
    mat[...] = base[...] + dot3(near, split(change))
    intensity = jnp.zeros((window, window), F32)
    for m in range(modes):
        far_real, far_imag = mat[0:window, lanes(m)], mat[window:, lanes(m)]
        intensity += far_real * far_real + far_imag * far_imag
    factor = (1.0 - jnp.sqrt(measured[0, 0] + 1.0) / jnp.sqrt(intensity + 1.0)) / window
    for m in range(modes):
        mat[0:window, lanes(m)] = mat[0:window, lanes(m)] * factor
        mat[window:, lanes(m)] = mat[window:, lanes(m)] * factor
    mat[...] = dot3(left_t, split(mat[...]))
    for m in range(modes):
        wide[lanes(m), 0:window] = mat[0:window, lanes(m)]
        wide[lanes(m), window:] = mat[window:, lanes(m)]
    wide[...] = dot3(split(wide[...]), left)

    tiles = window // 8
    shape = (tiles, 8, window)
    part = (depth // 4, 8, window)
    grad_real = jnp.zeros((band, window), F32)
    grad_imag = jnp.zeros((band, window), F32)
    for m in range(modes):
        first = m * window
        at = 2 * m * tiles
        acc[at : at + tiles] = wide[lanes(m), 0:window].reshape(shape) * 0.0625
        acc[at + tiles : at + 2 * tiles] = wide[lanes(m), window:].reshape(shape) * 0.0625
        middle = slice(first + low, first + high)
        back_real, back_imag = wide[middle, 0:window], wide[middle, window:]
        top_tile, end_tile = at + low // 8, at + high // 8
        acc[top_tile:end_tile] = (obj_real * back_real + obj_imag * back_imag).reshape(part) * 0.0625
        acc[top_tile + tiles : end_tile + tiles] = (
            obj_real * back_imag - obj_imag * back_real
        ).reshape(part) * 0.0625
    reducer = Reducer({"angle": a, "gz": g}, plan, acc, land, summed, (reduce_send, reduce_recv))
    reducer.begin()

    for m in range(modes):
        middle = slice(m * window + low, m * window + high)
        back_real, back_imag = wide[middle, 0:window], wide[middle, window:]
        mid_real, mid_imag = probe[m, 0, low:high], probe[m, 1, low:high]
        grad_real += mid_real * back_real + mid_imag * back_imag
        grad_imag += mid_real * back_imag - mid_imag * back_real
    patch_grad = grad_imag * obj_real - grad_real * obj_imag
    full = exact_dot(exact_dot(place_t, patch_grad), pick_t)
    for z in range(depth):
        sent[z] = full[z : z + 1]
    copies = []
    for d in range(1, depth):
        peer = lax.rem(g + d, depth)
        copies.append(push(sent.at[peer], received.at[g], rs.at[d], rr.at[d], (a, peer)))
        copies[-1].start()
    received[g] = sent[g]
    reducer.advance()
    for copy in copies:
        copy.wait()
    total = received[0]
    for z in range(1, depth):
        total = total + received[z]
    angle_sent[:, 0:width] = total
    angle_sent[:, width:] = jnp.zeros((1, 128), F32) + number[0].astype(F32)
    copies = []
    for d in range(1, angles):
        copies.append(push(angle_sent, angle_rows.at[a], as_.at[d], ar.at[d], (lax.rem(a + d, angles), g)))
        copies[-1].start()
    angle_rows[a] = angle_sent[...]
    for copy in copies:
        copy.wait()
    for load in loads:
        load.wait()

    block = width // 2
    work = []
    for c in range(2):
        cols = slice(c * block, (c + 1) * block)
        for j in range(angles):
            if c == 0:
                work.append(functools.partial(back_columns, j, angle_rows, wave, weights))
            work.append(functools.partial(back_part, j, cols, weights, rot, mix_t, wave, field))

        def finish(cols):
            out[0, :, cols] = 4.0 * dot3((fx_t[0], fx_t[1]), split(field[:, cols]))

        work.append(functools.partial(finish, cols))
    steps = 2 * reducer.stages - 1
    done = 0
    for step in range(steps):
        until = min(len(work), -(-len(work) * (step + 1) // (steps - 1)))
        for task in work[done:until]:
            task()
        done = until
        reducer.advance()
    probe_out[...] = summed[...]


def local(volume, probe, measured, angle_index, row_offset, col_offset):
    _, nx, ny = volume.shape
    modes, _, window, _ = probe.shape
    depth, angles = lax.axis_size("gz"), lax.axis_size("angle")
    rot, mix = angle_tables(nx, ny, angles)
    mix_pair = split_table(mix)
    mix_t_pair = split_table(np.swapaxes(mix, 1, 2))
    fx = packed_forward(nx)
    fx_pair, fx_t_pair = split_table(fx), split_table(fx.T)
    wave = wave_tables(ny)
    turns = 2.0 * np.pi * (np.arange(window)[:, None] * np.arange(window)[None, :] % window) / window
    cosine, sine = np.cos(turns), np.sin(turns)
    left = np.block([[cosine, sine], [-sine, cosine]])
    turn = np.stack([split_table(left), split_table(left.T)])
    big = 60 * 1024 * 1024
    hbm = pl.BlockSpec(memory_space=pl.ANY)

    row = pl.pallas_call(
        forward_kernel,
        in_specs=[SM] + [hbm] * 5,
        out_specs=VM,
        scratch_shapes=[
            pltpu.VMEM((1, nx, ny), BF16),
            pltpu.VMEM(fx_pair.shape, BF16),
            pltpu.VMEM((1, 2, nx // 2, ny), F32),
            pltpu.VMEM((2, 1, ny, nx), BF16),
            pltpu.VMEM(wave.shape, F32),
            pltpu.SemaphoreType.DMA((5,)),
        ],
        out_shape=jax.ShapeDtypeStruct((1, ny), F32),
        compiler_params=pltpu.CompilerParams(vmem_limit_bytes=big),
        name="forward",
    )(angle_index, volume, fx_pair, rot, mix_pair, wave)

    dma = pltpu.SemaphoreType.DMA
    block_rows = nx // angles
    tiles = modes * 2 * window // 8
    plan = reduce_plan(angles, depth, tiles)
    stages = 2 * len(plan[0][0])
    out, probe_total = pl.pallas_call(
        functools.partial(window_kernel, modes, plan),
        out_shape=(
            jax.ShapeDtypeStruct((1, block_rows, ny), F32),
            jax.ShapeDtypeStruct((tiles, 8, window), F32),
        ),
        in_specs=[SM, SM, SM, VM] + [hbm] * 7,
        out_specs=(VM, VM),
        scratch_shapes=[
            pltpu.VMEM((depth, 1, ny), F32),
            pltpu.VMEM((depth, 1, ny), F32),
            pltpu.VMEM((depth, 1, ny), F32),
            pltpu.VMEM((1, ny + 128), F32),
            pltpu.VMEM((angles, 1, ny + 128), F32),
            pltpu.VMEM((2 * window, modes * window), F32),
            pltpu.VMEM((modes * window, 2 * window), F32),
            pltpu.VMEM(probe.shape, F32),
            pltpu.VMEM(measured.shape, F32),
            pltpu.VMEM(turn.shape, BF16),
            pltpu.VMEM((2 * window, modes * window), F32),
            pltpu.VMEM((modes * 2 * depth, 2 * window), F32),
            pltpu.VMEM((angles, 2, ny // 2, 1), F32),
            pltpu.VMEM(wave.shape, F32),
            pltpu.VMEM(rot.shape, F32),
            pltpu.VMEM(mix_t_pair.shape, BF16),
            pltpu.VMEM((2, block_rows, nx), BF16),
            pltpu.VMEM((nx, ny), F32),
            pltpu.VMEM((tiles, 8, window), F32),
            pltpu.VMEM((tiles, 8, window), F32),
            pltpu.VMEM((tiles, 8, window), F32),
            dma((depth,)), dma((depth,)), dma((depth,)), dma((depth,)), dma((angles,)), dma((angles,)),
            dma((7,)), dma((stages, len(plan))), dma((stages, len(plan))),
        ],
        compiler_params=pltpu.CompilerParams(
            collective_id=0, has_side_effects=True, vmem_limit_bytes=48 * 1024 * 1024
        ),
        name="window",
    )(row_offset, col_offset, angle_index, row, probe, measured, turn, wave, rot, mix_t_pair, fx_t_pair)
    return (out, probe_total.reshape(probe.shape))


def solution(mesh):
    return jax.shard_map(
        local,
        mesh=mesh,
        in_specs=(
            P("gz", None, None),
            P(),
            P("angle", "gz", None, None),
            P("angle"),
            P("angle", "gz"),
            P("angle", "gz"),
        ),
        out_specs=(P("gz", "angle", None), P()),
        check_vma=False,
    )
```

```python
import functools
import math

import jax
import jax.numpy as jnp
import numpy as np
from jax import lax
from jax.experimental import pallas as pl
from jax.experimental.pallas import tpu as pltpu
from jax.sharding import PartitionSpec as P

MESH = pl.DeviceIdType.MESH
F32 = jnp.float32
BF16 = jnp.bfloat16
VM = pl.BlockSpec(memory_space=pltpu.VMEM)
SM = pl.BlockSpec(memory_space=pltpu.SMEM)


def split_table(table):
    table = np.asarray(table, np.float32)
    high = table.astype(jnp.bfloat16)
    low = (table - high.astype(np.float32)).astype(jnp.bfloat16)
    return np.stack([high, low])


def split(value):
    high = value.astype(BF16)
    return high, (value - high.astype(F32)).astype(BF16)


def dot(a, b):
    return jnp.dot(a, b, preferred_element_type=F32)


def dot3(a, b):
    return dot(a[0], b[0]) + (dot(a[0], b[1]) + dot(a[1], b[0]))


def packed_forward(n):
    k = np.arange(n // 2)[:, None]
    x = np.arange(n)[None, :]
    turns = 2.0 * np.pi * (k * x % n) / n
    imag = -np.sin(turns)
    imag[0] = np.where(x[0] % 2 == 0, 1.0, -1.0)
    return np.concatenate([np.cos(turns), imag], axis=0)


FINE = 16


def phase_table(unit, nyquist, count):
    rows = np.arange(FINE)[:, None]
    coarse = np.arange(count // 2 // FINE)[:, None] * FINE
    table = np.zeros((5, max(FINE, coarse.shape[0]), unit.shape[0]))
    for at, steps in ((0, coarse), (2, rows)):
        table[at, : len(steps)] = np.cos(steps * unit)
        table[at + 1, : len(steps)] = np.sin(steps * unit)
    table[4, 0] = nyquist
    return table.astype(np.float32)


def expand(small, full):
    fine_cos, fine_sin = small[2, 0:FINE], small[3, 0:FINE]
    for a in range(full.shape[1] // FINE):
        coarse_cos, coarse_sin = small[0, a : a + 1], small[1, a : a + 1]
        rows = slice(a * FINE, (a + 1) * FINE)
        full[0, rows] = coarse_cos * fine_cos - coarse_sin * fine_sin
        full[1, rows] = coarse_sin * fine_cos + coarse_cos * fine_sin
    full[1, 0:1] = small[4, 0:1]


def wave_tables(n):
    y = np.arange(n)
    return phase_table(2.0 * np.pi * y / n, np.where(y % 2 == 0, 1.0, -1.0), n)


def angle_tables(nx, ny, count):
    rot, mix = [], []
    cells_y = np.arange(ny)[None, :] - ny / 2
    cells_x = np.arange(nx)[None, :] - nx / 2
    weight = np.full(nx // 2, 2.0 / nx)
    weight[0] = 1.0 / nx
    for number in range(count):
        theta = math.pi * (number + 0.5) / count - math.pi / 2
        shear_x = -math.tan(theta / 2)
        shear_y = math.sin(theta)
        unit = -2.0 * np.pi * shear_x * cells_y[0] / nx
        rot.append(phase_table(unit, np.cos(unit * (nx // 2)), nx))
        ky = np.arange(ny // 2)[:, None]
        two = -2.0 * np.pi * ky * shear_y * cells_x / ny
        nyquist_two = 2.0 * np.pi * (ny // 2) * shear_y * cells_x[0] / ny
        upper, lower = np.cos(two), np.sin(two)
        lower[0] = np.cos(nyquist_two)
        spectrum = np.fft.rfft(np.concatenate([upper, lower], axis=0), axis=1)
        real = spectrum.real[:, : nx // 2] * weight
        imag = spectrum.imag[:, : nx // 2] * weight
        imag[:, 0] = spectrum.real[:, nx // 2] / nx
        mix.append(np.concatenate([real, imag], axis=1))
    return np.stack(rot), np.stack(mix)


def first_row(shape):
    return lax.broadcasted_iota(jnp.int32, shape, 0) == 0


def half_weights(n):
    return jnp.where(first_row((n // 2, 1)), 1.0 / n, 2.0 / n).astype(F32)


def forward_kernel(number, volume_hbm, fx_hbm, rot_hbm, mix_hbm, wave_hbm, out, volume, fx, rot_small, mix, wave_small, rot, wave, sems):
    angle = number[0]
    loads = [
        pltpu.make_async_copy(volume_hbm, volume, sems.at[0]),
        pltpu.make_async_copy(fx_hbm, fx, sems.at[1]),
        pltpu.make_async_copy(rot_hbm.at[pl.ds(angle, 1)], rot_small, sems.at[2]),
        pltpu.make_async_copy(mix_hbm.at[:, pl.ds(angle, 1)], mix, sems.at[3]),
        pltpu.make_async_copy(wave_hbm, wave_small, sems.at[4]),
    ]
    for at in (2, 4, 0, 1, 3):
        loads[at].start()
    n = volume.shape[1]
    half = n // 2
    loads[2].wait()
    expand(rot_small.at[0], rot.at[0])
    loads[4].wait()
    expand(wave_small, wave)
    loads[0].wait()
    loads[1].wait()
    field = volume[0]
    spec = dot(fx[0], field) + dot(fx[1], field)
    real, imag = spec[:half], spec[half:]
    top = first_row((half, 1))
    cosine, raw = rot[0, 0], rot[0, 1]
    sine = jnp.where(top, 0.0, raw)
    turned = jnp.concatenate(
        [real * cosine - imag * sine, real * sine + imag * jnp.where(top, raw, cosine)], axis=0
    )
    loads[3].wait()
    beam = dot3((mix[0, 0], mix[1, 0]), split(turned))
    upper, lower = beam[:half], beam[half:]
    cosine, raw = wave[0], wave[1]
    sine = jnp.where(top, 0.0, raw)
    weight = half_weights(wave.shape[2])
    sum_real = weight * jnp.sum(upper * cosine + lower * sine, axis=1, keepdims=True)
    sum_imag = weight * jnp.sum(
        lower * jnp.where(top, raw, cosine) - upper * sine, axis=1, keepdims=True
    )
    out[...] = jnp.sum(
        sum_real * cosine - sum_imag * jnp.where(top, -raw, raw), axis=0, keepdims=True
    )


def exact_dot(a, b):
    return jnp.dot(a, b, precision=lax.Precision.HIGHEST, preferred_element_type=F32)


def reduce_plan(angles, depth, tiles):
    angle_bits = [("angle", b) for b in range(angles.bit_length() - 1)]
    gz_bits = [("gz", b) for b in range(1, depth.bit_length() - 1)]
    core = [("gz", 0)]
    along_x = core + angle_bits + gz_bits
    along_y = core + angle_bits[::-1] + gz_bits
    z_then_x = core + gz_bits + angle_bits
    z_then_y = core + gz_bits + angle_bits[::-1]
    unit = angles * depth
    if tiles != 8 * unit:
        return [(along_x, tiles)]
    return [
        (along_x, 2 * unit), (along_y, 2 * unit), (z_then_x, unit),
        (z_then_y, unit), (along_x, unit), (along_y, unit),
    ]


class Reducer:
    def __init__(self, place, plan, acc, land, total, sems):
        self.place, self.acc, self.land, self.total = place, acc, land, total
        self.sems = sems
        self.plan = [order for order, _ in plan]
        self.length = [size for _, size in plan]
        self.start = [sum(self.length[:i]) for i in range(len(plan))]
        self.offset = list(self.start)
        self.stages = len(self.plan[0])
        self.flying = []

    def partner(self, axis, bit):
        index = self.place[axis]
        mine = lax.rem(index // (1 << bit), 2)
        other = dict(self.place)
        other[axis] = index + (1 - 2 * mine) * (1 << bit)
        return mine, (other["angle"], other["gz"])

    def copy(self, src, dst, stage, stream, device):
        send, recv = self.sems
        made = pltpu.make_async_remote_copy(
            src_ref=src, dst_ref=dst, send_sem=send.at[stage, stream], recv_sem=recv.at[stage, stream],
            device_id=device, device_id_type=MESH,
        )
        made.start()
        return made

    def start_halving(self, stage, i):
        mine, device = self.partner(*self.plan[i][stage])
        size = self.length[i] // 2
        keep = self.start[i] + mine * size
        other = self.start[i] + (1 - mine) * size
        landing = pl.ds(self.offset[i], size)
        made = self.copy(self.acc.at[pl.ds(other, size)], self.land.at[landing], stage, i, device)
        self.flying.append((made, keep, size, landing))

    def start_doubling(self, stage, i):
        mine, device = self.partner(*self.plan[i][2 * self.stages - 1 - stage])
        rows = self.total.at[pl.ds(self.start[i], self.length[i])]
        made = self.copy(rows, rows, stage, i, device)
        self.start[i] = self.start[i] - mine * self.length[i]
        self.length[i] *= 2
        self.flying.append((made,))

    def begin(self):
        self.stage = 0
        for i in range(len(self.plan)):
            self.start_halving(0, i)

    def advance(self):
        flying, self.flying = self.flying, []
        after = self.stage + 1
        for i, (made, *rest) in enumerate(flying):
            made.wait()
            if self.stage < self.stages:
                keep, size, landing = rest
                rows = pl.ds(keep, size)
                into = self.acc if after < self.stages else self.total
                into[rows] = self.acc[rows] + self.land[landing]
                self.start[i], self.length[i] = keep, size
                self.offset[i] += size
            if after < self.stages:
                self.start_halving(after, i)
            elif after < 2 * self.stages:
                self.start_doubling(after, i)
        self.stage = after


def back_columns(j, angle_rows, wave, weights, rot_small, rot):
    if j > 0:
        expand(rot_small.at[j], rot.at[j])
    half, width = wave.shape[1], wave.shape[2]
    row = jnp.zeros((1, width), F32)
    for a in range(angle_rows.shape[0]):
        mine = angle_rows[a, :, width : width + 1] == float(j)
        row = row + jnp.where(mine, angle_rows[a, :, 0:width], 0.0)
    cosine, raw = wave[0], wave[1]
    top = first_row((half, 1))
    weight = half_weights(width)
    weights[j, 0] = weight * jnp.sum(row * cosine, axis=1, keepdims=True)
    weights[j, 1] = -weight * jnp.sum(row * jnp.where(top, -raw, raw), axis=1, keepdims=True)


def back_part(j, cols, weights, rot, mix_t, wave, acc):
    in_real, in_imag = weights[j, 0], weights[j, 1]
    cosine, raw = wave[0, :, cols], wave[1, :, cols]
    top = first_row((cosine.shape[0], 1))
    sine = jnp.where(top, 0.0, raw)
    beam = jnp.concatenate(
        [in_real * cosine - in_imag * sine, in_real * sine + in_imag * jnp.where(top, raw, cosine)], axis=0
    )
    turned = dot3((mix_t[0, j], mix_t[1, j]), split(beam))
    kx = turned.shape[0] // 2
    real, imag = turned[:kx], turned[kx:]
    top = first_row((kx, 1))
    cosine, raw = rot[j, 0, :, cols], rot[j, 1, :, cols]
    sine = jnp.where(top, 0.0, raw)
    upper = real * cosine + imag * sine
    lower = imag * jnp.where(top, raw, cosine) - real * sine
    if j > 0:
        upper, lower = acc[:kx, cols] + upper, acc[kx:, cols] + lower
    acc[:kx, cols] = upper
    acc[kx:, cols] = lower


def window_kernel(
    modes, plan, row_off, col_off, number, row, probe_hbm, measured_hbm, turn_hbm, wave_hbm, rot_hbm, mix_hbm, fx_hbm,
    out, probe_out,
    gathered, sent, received, angle_sent, angle_rows, mat, wide, probe, measured, turn, base, thin, weights, wave_small, rot_small,
    wave, rot, mix_t, fx_t, field, acc, land, summed,
    gs, gr, rs, rr, as_, ar, tables, reduce_send, reduce_recv,
):
    depth, angles = gathered.shape[0], angle_rows.shape[0]
    width = row.shape[1]
    window = probe.shape[-1]
    half = window // 2
    g, a = lax.axis_index("gz"), lax.axis_index("angle")

    block_rows = fx_t.shape[1]
    early = [
        pltpu.make_async_copy(turn_hbm, turn, tables.at[4]),
        pltpu.make_async_copy(probe_hbm, probe, tables.at[5]),
        pltpu.make_async_copy(measured_hbm, measured, tables.at[6]),
    ]
    for load in early:
        load.start()
    loads = [
        pltpu.make_async_copy(wave_hbm, wave_small, tables.at[0]),
        pltpu.make_async_copy(rot_hbm, rot_small, tables.at[1]),
        pltpu.make_async_copy(mix_hbm, mix_t, tables.at[2]),
        pltpu.make_async_copy(fx_hbm.at[:, pl.ds(a * block_rows, block_rows)], fx_t, tables.at[3]),
    ]
    barrier = pltpu.get_barrier_semaphore()
    for d in range(1, depth):
        pl.semaphore_signal(barrier, inc=1, device_id=(a, lax.rem(g + d, depth)), device_id_type=MESH)
    for d in range(1, angles):
        pl.semaphore_signal(barrier, inc=1, device_id=(lax.rem(a + d, angles), g), device_id_type=MESH)
    pl.semaphore_wait(barrier, depth + angles - 2)

    def push(src, dst, send, recv, device):
        return pltpu.make_async_remote_copy(
            src_ref=src, dst_ref=dst, send_sem=send, recv_sem=recv, device_id=device, device_id_type=MESH
        )

    copies = []
    for d in range(1, depth):
        copies.append(push(row, gathered.at[g], gs.at[d], gr.at[d], (a, lax.rem(g + d, depth))))
        copies[-1].start()
    gathered[g] = row[...]
    for load in early:
        load.wait()
    for load in loads:
        load.start()

    row0, col0 = row_off[0, 0], col_off[0, 0]
    iota = lax.broadcasted_iota
    pick = (iota(jnp.int32, (width, window), 0) == iota(jnp.int32, (width, window), 1) + col0).astype(F32)
    pick_t = (iota(jnp.int32, (window, width), 1) == iota(jnp.int32, (window, width), 0) + col0).astype(F32)
    shape = (2 * depth, depth)
    place = (
        iota(jnp.int32, shape, 0) + (half - depth) == iota(jnp.int32, shape, 1) - row0
    ).astype(F32)
    place_t = (
        iota(jnp.int32, shape[::-1], 1) + (half - depth) == iota(jnp.int32, shape[::-1], 0) - row0
    ).astype(F32)
    low, high, band = half - depth, half + depth, 2 * depth
    left, left_t = (turn[0, 0], turn[0, 1]), (turn[1, 0], turn[1, 1])

    def lanes(m):
        return slice(m * window, (m + 1) * window)

    for m in range(modes):
        wide[lanes(m), 0:window] = probe[m, 0]
        wide[lanes(m), window:] = probe[m, 1]
    wide[...] = dot3(split(wide[...]), left_t)
    for m in range(modes):
        mat[0:window, lanes(m)] = wide[lanes(m), 0:window]
        mat[window:, lanes(m)] = wide[lanes(m), window:]
    base[...] = dot3(left, split(mat[...]))
    for copy in copies:
        copy.wait()

    rows = jnp.concatenate([gathered[z] for z in range(depth)], axis=0)
    patch = exact_dot(place, exact_dot(rows, pick))
    obj_real, obj_imag = jnp.cos(patch), jnp.sin(patch)
    for m in range(modes):
        mid_real, mid_imag = probe[m, 0, low:high], probe[m, 1, low:high]
        thin[m * band : (m + 1) * band, 0:window] = mid_real * obj_real - mid_imag * obj_imag - mid_real
        thin[m * band : (m + 1) * band, window:] = mid_real * obj_imag + mid_imag * obj_real - mid_imag
    change = dot3(split(thin[...]), left_t)
    change = jnp.concatenate(
        [
            jnp.concatenate([change[m * band : (m + 1) * band, c : c + window] for m in range(modes)], axis=1)
            for c in (0, window)
        ],
        axis=0,
    )
    near = tuple(
        jnp.concatenate([part[:, low:high], part[:, window + low : window + high]], axis=1) for part in left
    )
    mat[...] = base[...] + dot3(near, split(change))
    intensity = jnp.zeros((window, window), F32)
    for m in range(modes):
        far_real, far_imag = mat[0:window, lanes(m)], mat[window:, lanes(m)]
        intensity += far_real * far_real + far_imag * far_imag
    factor = (1.0 - jnp.sqrt(measured[0, 0] + 1.0) / jnp.sqrt(intensity + 1.0)) / window
    for m in range(modes):
        mat[0:window, lanes(m)] = mat[0:window, lanes(m)] * factor
        mat[window:, lanes(m)] = mat[window:, lanes(m)] * factor
    mat[...] = dot3(left_t, split(mat[...]))
    for m in range(modes):
        wide[lanes(m), 0:window] = mat[0:window, lanes(m)]
        wide[lanes(m), window:] = mat[window:, lanes(m)]
    wide[...] = dot3(split(wide[...]), left)

    tiles = window // 8
    shape = (tiles, 8, window)
    part = (depth // 4, 8, window)
    grad_real = jnp.zeros((band, window), F32)
    grad_imag = jnp.zeros((band, window), F32)
    for m in range(modes):
        first = m * window
        at = 2 * m * tiles
        acc[at : at + tiles] = wide[lanes(m), 0:window].reshape(shape) * 0.0625
        acc[at + tiles : at + 2 * tiles] = wide[lanes(m), window:].reshape(shape) * 0.0625
        middle = slice(first + low, first + high)
        back_real, back_imag = wide[middle, 0:window], wide[middle, window:]
        top_tile, end_tile = at + low // 8, at + high // 8
        acc[top_tile:end_tile] = (obj_real * back_real + obj_imag * back_imag).reshape(part) * 0.0625
        acc[top_tile + tiles : end_tile + tiles] = (
            obj_real * back_imag - obj_imag * back_real
        ).reshape(part) * 0.0625
    reducer = Reducer({"angle": a, "gz": g}, plan, acc, land, summed, (reduce_send, reduce_recv))
    reducer.begin()

    for m in range(modes):
        middle = slice(m * window + low, m * window + high)
        back_real, back_imag = wide[middle, 0:window], wide[middle, window:]
        mid_real, mid_imag = probe[m, 0, low:high], probe[m, 1, low:high]
        grad_real += mid_real * back_real + mid_imag * back_imag
        grad_imag += mid_real * back_imag - mid_imag * back_real
    patch_grad = grad_imag * obj_real - grad_real * obj_imag
    full = exact_dot(exact_dot(place_t, patch_grad), pick_t)
    for z in range(depth):
        sent[z] = full[z : z + 1]
    copies = []
    for d in range(1, depth):
        peer = lax.rem(g + d, depth)
        copies.append(push(sent.at[peer], received.at[g], rs.at[d], rr.at[d], (a, peer)))
        copies[-1].start()
    received[g] = sent[g]
    for load in loads:
        load.wait()
    reducer.advance()
    expand(wave_small, wave)
    for copy in copies:
        copy.wait()
    total = received[0]
    for z in range(1, depth):
        total = total + received[z]
    angle_sent[:, 0:width] = total
    angle_sent[:, width:] = jnp.zeros((1, 128), F32) + number[0].astype(F32)
    copies = []
    for d in range(1, angles):
        copies.append(push(angle_sent, angle_rows.at[a], as_.at[d], ar.at[d], (lax.rem(a + d, angles), g)))
        copies[-1].start()
    angle_rows[a] = angle_sent[...]
    expand(rot_small.at[0], rot.at[0])
    reducer.advance()
    for copy in copies:
        copy.wait()

    block = width // 2
    work = []
    for c in range(2):
        cols = slice(c * block, (c + 1) * block)
        for j in range(angles):
            if c == 0:
                work.append(functools.partial(back_columns, j, angle_rows, wave, weights, rot_small, rot))
            work.append(functools.partial(back_part, j, cols, weights, rot, mix_t, wave, field))

        def finish(cols):
            out[0, :, cols] = 4.0 * dot3((fx_t[0], fx_t[1]), split(field[:, cols]))

        work.append(functools.partial(finish, cols))
    steps = 2 * reducer.stages - 2
    share = [1] * steps
    share[0] = share[-3] = 3
    share[-2], share[-1] = 4, 0
    done = 0
    for step in range(steps):
        until = -(-len(work) * sum(share[: step + 1]) // sum(share))
        for task in work[done:until]:
            task()
        done = until
        reducer.advance()
    probe_out[...] = summed[...]


def local(volume, probe, measured, angle_index, row_offset, col_offset):
    _, nx, ny = volume.shape
    modes, _, window, _ = probe.shape
    depth, angles = lax.axis_size("gz"), lax.axis_size("angle")
    rot, mix = angle_tables(nx, ny, angles)
    mix_pair = split_table(mix)
    mix_t_pair = split_table(np.swapaxes(mix, 1, 2))
    fx = packed_forward(nx)
    fx_pair, fx_t_pair = split_table(fx), split_table(fx.T)
    wave = wave_tables(ny)
    turns = 2.0 * np.pi * (np.arange(window)[:, None] * np.arange(window)[None, :] % window) / window
    cosine, sine = np.cos(turns), np.sin(turns)
    left = np.block([[cosine, sine], [-sine, cosine]])
    turn = np.stack([split_table(left), split_table(left.T)])
    big = 60 * 1024 * 1024
    hbm = pl.BlockSpec(memory_space=pl.ANY)

    row = pl.pallas_call(
        forward_kernel,
        in_specs=[SM] + [hbm] * 5,
        out_specs=VM,
        scratch_shapes=[
            pltpu.VMEM((1, nx, ny), BF16),
            pltpu.VMEM(fx_pair.shape, BF16),
            pltpu.VMEM((1,) + rot.shape[1:], F32),
            pltpu.VMEM((2, 1, ny, nx), BF16),
            pltpu.VMEM(wave.shape, F32),
            pltpu.VMEM((1, 2, nx // 2, ny), F32),
            pltpu.VMEM((2, ny // 2, ny), F32),
            pltpu.SemaphoreType.DMA((5,)),
        ],
        out_shape=jax.ShapeDtypeStruct((1, ny), F32),
        compiler_params=pltpu.CompilerParams(vmem_limit_bytes=big),
        name="forward",
    )(angle_index, volume, fx_pair, rot, mix_pair, wave)

    dma = pltpu.SemaphoreType.DMA
    block_rows = nx // angles
    tiles = modes * 2 * window // 8
    plan = reduce_plan(angles, depth, tiles)
    stages = 2 * len(plan[0][0])
    out, probe_total = pl.pallas_call(
        functools.partial(window_kernel, modes, plan),
        out_shape=(
            jax.ShapeDtypeStruct((1, block_rows, ny), F32),
            jax.ShapeDtypeStruct((tiles, 8, window), F32),
        ),
        in_specs=[SM, SM, SM, VM] + [hbm] * 7,
        out_specs=(VM, VM),
        scratch_shapes=[
            pltpu.VMEM((depth, 1, ny), F32),
            pltpu.VMEM((depth, 1, ny), F32),
            pltpu.VMEM((depth, 1, ny), F32),
            pltpu.VMEM((1, ny + 128), F32),
            pltpu.VMEM((angles, 1, ny + 128), F32),
            pltpu.VMEM((2 * window, modes * window), F32),
            pltpu.VMEM((modes * window, 2 * window), F32),
            pltpu.VMEM(probe.shape, F32),
            pltpu.VMEM(measured.shape, F32),
            pltpu.VMEM(turn.shape, BF16),
            pltpu.VMEM((2 * window, modes * window), F32),
            pltpu.VMEM((modes * 2 * depth, 2 * window), F32),
            pltpu.VMEM((angles, 2, ny // 2, 1), F32),
            pltpu.VMEM(wave.shape, F32),
            pltpu.VMEM(rot.shape, F32),
            pltpu.VMEM((2, ny // 2, ny), F32),
            pltpu.VMEM((angles, 2, nx // 2, ny), F32),
            pltpu.VMEM(mix_t_pair.shape, BF16),
            pltpu.VMEM((2, block_rows, nx), BF16),
            pltpu.VMEM((nx, ny), F32),
            pltpu.VMEM((tiles, 8, window), F32),
            pltpu.VMEM((tiles, 8, window), F32),
            pltpu.VMEM((tiles, 8, window), F32),
            dma((depth,)), dma((depth,)), dma((depth,)), dma((depth,)), dma((angles,)), dma((angles,)),
            dma((7,)), dma((stages, len(plan))), dma((stages, len(plan))),
        ],
        compiler_params=pltpu.CompilerParams(
            collective_id=0, has_side_effects=True, vmem_limit_bytes=48 * 1024 * 1024
        ),
        name="window",
    )(row_offset, col_offset, angle_index, row, probe, measured, turn, wave, rot, mix_t_pair, fx_t_pair)
    return (out, probe_total.reshape(probe.shape))


def solution(mesh):
    return jax.shard_map(
        local,
        mesh=mesh,
        in_specs=(
            P("gz", None, None),
            P(),
            P("angle", "gz", None, None),
            P("angle"),
            P("angle", "gz"),
            P("angle", "gz"),
        ),
        out_specs=(P("gz", "angle", None), P()),
        check_vma=False,
    )
```

```python
import functools
import math

import jax
import jax.numpy as jnp
import numpy as np
from jax import lax
from jax.experimental import pallas as pl
from jax.experimental.pallas import tpu as pltpu
from jax.sharding import PartitionSpec as P

MESH = pl.DeviceIdType.MESH
F32 = jnp.float32
BF16 = jnp.bfloat16
VM = pl.BlockSpec(memory_space=pltpu.VMEM)
SM = pl.BlockSpec(memory_space=pltpu.SMEM)


def split_table(table):
    table = np.asarray(table, np.float32)
    high = table.astype(jnp.bfloat16)
    low = (table - high.astype(np.float32)).astype(jnp.bfloat16)
    return np.stack([high, low])


def split(value):
    high = value.astype(BF16)
    return high, (value - high.astype(F32)).astype(BF16)


def dot(a, b):
    return jnp.dot(a, b, preferred_element_type=F32)


def dot3(a, b):
    return dot(a[0], b[0]) + (dot(a[0], b[1]) + dot(a[1], b[0]))


def packed_forward(n):
    k = np.arange(n // 2)[:, None]
    x = np.arange(n)[None, :]
    turns = 2.0 * np.pi * (k * x % n) / n
    imag = -np.sin(turns)
    imag[0] = np.where(x[0] % 2 == 0, 1.0, -1.0)
    return np.concatenate([np.cos(turns), imag], axis=0)


FINE = 16


def phase_table(unit, nyquist, count):
    rows = np.arange(FINE)[:, None]
    coarse = np.arange(count // 2 // FINE)[:, None] * FINE
    table = np.zeros((5, max(FINE, coarse.shape[0]), unit.shape[0]))
    for at, steps in ((0, coarse), (2, rows)):
        table[at, : len(steps)] = np.cos(steps * unit)
        table[at + 1, : len(steps)] = np.sin(steps * unit)
    table[4, 0] = nyquist
    return table.astype(np.float32)


def expand(small, full):
    fine_cos, fine_sin = small[2, 0:FINE], small[3, 0:FINE]
    for a in range(full.shape[1] // FINE):
        coarse_cos, coarse_sin = small[0, a : a + 1], small[1, a : a + 1]
        rows = slice(a * FINE, (a + 1) * FINE)
        full[0, rows] = coarse_cos * fine_cos - coarse_sin * fine_sin
        full[1, rows] = coarse_sin * fine_cos + coarse_cos * fine_sin
    full[1, 0:1] = small[4, 0:1]


def wave_tables(n):
    y = np.arange(n)
    return phase_table(2.0 * np.pi * y / n, np.where(y % 2 == 0, 1.0, -1.0), n)


def angle_tables(nx, ny, count):
    rot, mix = [], []
    cells_y = np.arange(ny)[None, :] - ny / 2
    cells_x = np.arange(nx)[None, :] - nx / 2
    weight = np.full(nx // 2, 2.0 / nx)
    weight[0] = 1.0 / nx
    for number in range(count):
        theta = math.pi * (number + 0.5) / count - math.pi / 2
        shear_x = -math.tan(theta / 2)
        shear_y = math.sin(theta)
        unit = -2.0 * np.pi * shear_x * cells_y[0] / nx
        rot.append(phase_table(unit, np.cos(unit * (nx // 2)), nx))
        ky = np.arange(ny // 2)[:, None]
        two = -2.0 * np.pi * ky * shear_y * cells_x / ny
        nyquist_two = 2.0 * np.pi * (ny // 2) * shear_y * cells_x[0] / ny
        upper, lower = np.cos(two), np.sin(two)
        lower[0] = np.cos(nyquist_two)
        spectrum = np.fft.rfft(np.concatenate([upper, lower], axis=0), axis=1)
        real = spectrum.real[:, : nx // 2] * weight
        imag = spectrum.imag[:, : nx // 2] * weight
        imag[:, 0] = spectrum.real[:, nx // 2] / nx
        mix.append(np.concatenate([real, imag], axis=1))
    return np.stack(rot), np.stack(mix)


def first_row(shape):
    return lax.broadcasted_iota(jnp.int32, shape, 0) == 0


def half_weights(n):
    return jnp.where(first_row((n // 2, 1)), 1.0 / n, 2.0 / n).astype(F32)


def forward_kernel(number, volume_hbm, fx_hbm, rot_hbm, mix_hbm, wave_hbm, out, volume, fx, rot_small, mix, wave_small, rot, wave, sems):
    angle = number[0]
    loads = [
        pltpu.make_async_copy(volume_hbm, volume, sems.at[0]),
        pltpu.make_async_copy(fx_hbm, fx, sems.at[1]),
        pltpu.make_async_copy(rot_hbm.at[pl.ds(angle, 1)], rot_small, sems.at[2]),
        pltpu.make_async_copy(mix_hbm.at[:, pl.ds(angle, 1)], mix, sems.at[3]),
        pltpu.make_async_copy(wave_hbm, wave_small, sems.at[4]),
    ]
    for at in (2, 4, 0, 1, 3):
        loads[at].start()
    n = volume.shape[1]
    half = n // 2
    loads[2].wait()
    expand(rot_small.at[0], rot.at[0])
    loads[4].wait()
    expand(wave_small, wave)
    loads[0].wait()
    loads[1].wait()
    field = volume[0]
    spec = dot(fx[0], field) + dot(fx[1], field)
    real, imag = spec[:half], spec[half:]
    top = first_row((half, 1))
    cosine, raw = rot[0, 0], rot[0, 1]
    sine = jnp.where(top, 0.0, raw)
    turned = jnp.concatenate(
        [real * cosine - imag * sine, real * sine + imag * jnp.where(top, raw, cosine)], axis=0
    )
    loads[3].wait()
    beam = dot3((mix[0, 0], mix[1, 0]), split(turned))
    upper, lower = beam[:half], beam[half:]
    cosine, raw = wave[0], wave[1]
    sine = jnp.where(top, 0.0, raw)
    weight = half_weights(wave.shape[2])
    sum_real = weight * jnp.sum(upper * cosine + lower * sine, axis=1, keepdims=True)
    sum_imag = weight * jnp.sum(
        lower * jnp.where(top, raw, cosine) - upper * sine, axis=1, keepdims=True
    )
    out[...] = jnp.sum(
        sum_real * cosine - sum_imag * jnp.where(top, -raw, raw), axis=0, keepdims=True
    )


def exact_dot(a, b):
    return jnp.dot(a, b, precision=lax.Precision.HIGHEST, preferred_element_type=F32)


def reduce_plan(angles, depth, tiles):
    angle_bits = [("angle", 1 << b, 2) for b in range(angles.bit_length() - 1)]
    core = [("gz", 1, 2)]
    along_z = [("gz", 2, 4)] + [("gz", 1 << b, 2) for b in range(3, depth.bit_length() - 1)]
    along_x = core + angle_bits + along_z
    along_y = core + angle_bits[::-1] + along_z
    z_then_x = core + along_z + angle_bits
    z_then_y = core + along_z + angle_bits[::-1]
    unit = angles * depth
    if tiles != 8 * unit:
        return [(along_x, tiles)]
    return [
        (along_x, 2 * unit), (along_y, 2 * unit), (z_then_x, unit),
        (z_then_y, unit), (along_x, unit), (along_y, unit),
    ]


class Reducer:
    def __init__(self, place, plan, acc, land, total, sems):
        self.place, self.acc, self.land, self.total = place, acc, land, total
        self.sems = sems
        self.plan = [order for order, _ in plan]
        self.length = [size for _, size in plan]
        self.start = [sum(self.length[:i]) for i in range(len(plan))]
        self.offset = list(self.start)
        self.stages = len(self.plan[0])
        self.flying = []

    def partners(self, axis, unit, ways):
        index = self.place[axis]
        mine = lax.rem(index // unit, ways)
        found = []
        for mask in range(1, ways):
            piece = 0
            for b in range(ways.bit_length() - 1):
                bit = lax.rem(mine // (1 << b), 2)
                piece = piece + (1 << b) * (1 - bit if mask >> b & 1 else bit)
            other = dict(self.place)
            other[axis] = index + (piece - mine) * unit
            found.append((piece, (other["angle"], other["gz"])))
        return mine, found

    def copy(self, src, dst, stage, stream, lane, device):
        send, recv = self.sems
        made = pltpu.make_async_remote_copy(
            src_ref=src, dst_ref=dst, send_sem=send.at[stage, stream, lane], recv_sem=recv.at[stage, stream, lane],
            device_id=device, device_id_type=MESH,
        )
        made.start()
        return made

    def start_halving(self, stage, i):
        ways = self.plan[i][stage][2]
        mine, found = self.partners(*self.plan[i][stage])
        size = self.length[i] // ways
        made, landings = [], []
        for lane, (piece, device) in enumerate(found):
            landing = pl.ds(self.offset[i] + lane * size, size)
            other = pl.ds(self.start[i] + piece * size, size)
            made.append(self.copy(self.acc.at[other], self.land.at[landing], stage, i, lane, device))
            landings.append(landing)
        self.flying.append((made, self.start[i] + mine * size, size, landings))

    def start_doubling(self, stage, i):
        step = self.plan[i][2 * self.stages - 1 - stage]
        mine, found = self.partners(*step)
        rows = self.total.at[pl.ds(self.start[i], self.length[i])]
        made = [self.copy(rows, rows, stage, i, lane, device) for lane, (_, device) in enumerate(found)]
        self.start[i] = self.start[i] - mine * self.length[i]
        self.length[i] *= step[2]
        self.flying.append((made,))

    def begin(self):
        self.stage = 0
        for i in range(len(self.plan)):
            self.start_halving(0, i)

    def advance(self):
        flying, self.flying = self.flying, []
        after = self.stage + 1
        for i, (made, *rest) in enumerate(flying):
            for one in made:
                one.wait()
            if self.stage < self.stages:
                keep, size, landings = rest
                rows = pl.ds(keep, size)
                into = self.acc if after < self.stages else self.total
                value = self.acc[rows]
                for landing in landings:
                    value = value + self.land[landing]
                into[rows] = value
                self.start[i], self.length[i] = keep, size
                self.offset[i] += size * len(landings)
            if after < self.stages:
                self.start_halving(after, i)
            elif after < 2 * self.stages:
                self.start_doubling(after, i)
        self.stage = after


def back_columns(j, angle_rows, wave, weights, rot_small, rot):
    if j > 0:
        expand(rot_small.at[j], rot.at[j])
    half, width = wave.shape[1], wave.shape[2]
    row = jnp.zeros((1, width), F32)
    for a in range(angle_rows.shape[0]):
        mine = angle_rows[a, :, width : width + 1] == float(j)
        row = row + jnp.where(mine, angle_rows[a, :, 0:width], 0.0)
    cosine, raw = wave[0], wave[1]
    top = first_row((half, 1))
    weight = half_weights(width)
    weights[j, 0] = weight * jnp.sum(row * cosine, axis=1, keepdims=True)
    weights[j, 1] = -weight * jnp.sum(row * jnp.where(top, -raw, raw), axis=1, keepdims=True)


def back_part(j, cols, weights, rot, mix_t, wave, acc):
    in_real, in_imag = weights[j, 0], weights[j, 1]
    cosine, raw = wave[0, :, cols], wave[1, :, cols]
    top = first_row((cosine.shape[0], 1))
    sine = jnp.where(top, 0.0, raw)
    beam = jnp.concatenate(
        [in_real * cosine - in_imag * sine, in_real * sine + in_imag * jnp.where(top, raw, cosine)], axis=0
    )
    turned = dot3((mix_t[0, j], mix_t[1, j]), split(beam))
    kx = turned.shape[0] // 2
    real, imag = turned[:kx], turned[kx:]
    top = first_row((kx, 1))
    cosine, raw = rot[j, 0, :, cols], rot[j, 1, :, cols]
    sine = jnp.where(top, 0.0, raw)
    upper = real * cosine + imag * sine
    lower = imag * jnp.where(top, raw, cosine) - real * sine
    if j > 0:
        upper, lower = acc[:kx, cols] + upper, acc[kx:, cols] + lower
    acc[:kx, cols] = upper
    acc[kx:, cols] = lower


def window_kernel(
    modes, plan, row_off, col_off, number, row, probe_hbm, measured_hbm, turn_hbm, wave_hbm, rot_hbm, mix_hbm, fx_hbm,
    out, probe_out,
    gathered, sent, received, angle_sent, angle_rows, mat, wide, probe, measured, turn, base, thin, weights, wave_small, rot_small,
    wave, rot, mix_t, fx_t, field, acc, land, summed,
    gs, gr, rs, rr, as_, ar, tables, reduce_send, reduce_recv,
):
    depth, angles = gathered.shape[0], angle_rows.shape[0]
    width = row.shape[1]
    window = probe.shape[-1]
    half = window // 2
    g, a = lax.axis_index("gz"), lax.axis_index("angle")

    block_rows = fx_t.shape[1]
    early = [
        pltpu.make_async_copy(turn_hbm, turn, tables.at[4]),
        pltpu.make_async_copy(probe_hbm, probe, tables.at[5]),
        pltpu.make_async_copy(measured_hbm, measured, tables.at[6]),
    ]
    for load in early:
        load.start()
    loads = [
        pltpu.make_async_copy(wave_hbm, wave_small, tables.at[0]),
        pltpu.make_async_copy(rot_hbm, rot_small, tables.at[1]),
        pltpu.make_async_copy(mix_hbm, mix_t, tables.at[2]),
        pltpu.make_async_copy(fx_hbm.at[:, pl.ds(a * block_rows, block_rows)], fx_t, tables.at[3]),
    ]
    barrier = pltpu.get_barrier_semaphore()
    for d in range(1, depth):
        pl.semaphore_signal(barrier, inc=1, device_id=(a, lax.rem(g + d, depth)), device_id_type=MESH)
    for d in range(1, angles):
        pl.semaphore_signal(barrier, inc=1, device_id=(lax.rem(a + d, angles), g), device_id_type=MESH)
    pl.semaphore_wait(barrier, depth + angles - 2)

    def push(src, dst, send, recv, device):
        return pltpu.make_async_remote_copy(
            src_ref=src, dst_ref=dst, send_sem=send, recv_sem=recv, device_id=device, device_id_type=MESH
        )

    copies = []
    for d in range(1, depth):
        copies.append(push(row, gathered.at[g], gs.at[d], gr.at[d], (a, lax.rem(g + d, depth))))
        copies[-1].start()
    gathered[g] = row[...]
    for load in early:
        load.wait()
    for load in loads:
        load.start()

    row0, col0 = row_off[0, 0], col_off[0, 0]
    iota = lax.broadcasted_iota
    pick = (iota(jnp.int32, (width, window), 0) == iota(jnp.int32, (width, window), 1) + col0).astype(F32)
    pick_t = (iota(jnp.int32, (window, width), 1) == iota(jnp.int32, (window, width), 0) + col0).astype(F32)
    shape = (2 * depth, depth)
    place = (
        iota(jnp.int32, shape, 0) + (half - depth) == iota(jnp.int32, shape, 1) - row0
    ).astype(F32)
    place_t = (
        iota(jnp.int32, shape[::-1], 1) + (half - depth) == iota(jnp.int32, shape[::-1], 0) - row0
    ).astype(F32)
    low, high, band = half - depth, half + depth, 2 * depth
    left, left_t = (turn[0, 0], turn[0, 1]), (turn[1, 0], turn[1, 1])

    def lanes(m):
        return slice(m * window, (m + 1) * window)

    for m in range(modes):
        wide[lanes(m), 0:window] = probe[m, 0]
        wide[lanes(m), window:] = probe[m, 1]
    wide[...] = dot3(split(wide[...]), left_t)
    for m in range(modes):
        mat[0:window, lanes(m)] = wide[lanes(m), 0:window]
        mat[window:, lanes(m)] = wide[lanes(m), window:]
    base[...] = dot3(left, split(mat[...]))
    for copy in copies:
        copy.wait()

    rows = jnp.concatenate([gathered[z] for z in range(depth)], axis=0)
    patch = exact_dot(place, exact_dot(rows, pick))
    obj_real, obj_imag = jnp.cos(patch), jnp.sin(patch)
    for m in range(modes):
        mid_real, mid_imag = probe[m, 0, low:high], probe[m, 1, low:high]
        thin[m * band : (m + 1) * band, 0:window] = mid_real * obj_real - mid_imag * obj_imag - mid_real
        thin[m * band : (m + 1) * band, window:] = mid_real * obj_imag + mid_imag * obj_real - mid_imag
    change = dot3(split(thin[...]), left_t)
    change = jnp.concatenate(
        [
            jnp.concatenate([change[m * band : (m + 1) * band, c : c + window] for m in range(modes)], axis=1)
            for c in (0, window)
        ],
        axis=0,
    )
    near = tuple(
        jnp.concatenate([part[:, low:high], part[:, window + low : window + high]], axis=1) for part in left
    )
    mat[...] = base[...] + dot3(near, split(change))
    intensity = jnp.zeros((window, window), F32)
    for m in range(modes):
        far_real, far_imag = mat[0:window, lanes(m)], mat[window:, lanes(m)]
        intensity += far_real * far_real + far_imag * far_imag
    factor = (1.0 - jnp.sqrt(measured[0, 0] + 1.0) / jnp.sqrt(intensity + 1.0)) / window
    for m in range(modes):
        mat[0:window, lanes(m)] = mat[0:window, lanes(m)] * factor
        mat[window:, lanes(m)] = mat[window:, lanes(m)] * factor
    mat[...] = dot3(left_t, split(mat[...]))
    for m in range(modes):
        wide[lanes(m), 0:window] = mat[0:window, lanes(m)]
        wide[lanes(m), window:] = mat[window:, lanes(m)]
    wide[...] = dot3(split(wide[...]), left)

    tiles = window // 8
    shape = (tiles, 8, window)
    part = (depth // 4, 8, window)
    grad_real = jnp.zeros((band, window), F32)
    grad_imag = jnp.zeros((band, window), F32)
    for m in range(modes):
        first = m * window
        at = 2 * m * tiles
        acc[at : at + tiles] = wide[lanes(m), 0:window].reshape(shape) * 0.0625
        acc[at + tiles : at + 2 * tiles] = wide[lanes(m), window:].reshape(shape) * 0.0625
        middle = slice(first + low, first + high)
        back_real, back_imag = wide[middle, 0:window], wide[middle, window:]
        top_tile, end_tile = at + low // 8, at + high // 8
        acc[top_tile:end_tile] = (obj_real * back_real + obj_imag * back_imag).reshape(part) * 0.0625
        acc[top_tile + tiles : end_tile + tiles] = (
            obj_real * back_imag - obj_imag * back_real
        ).reshape(part) * 0.0625
    reducer = Reducer({"angle": a, "gz": g}, plan, acc, land, summed, (reduce_send, reduce_recv))
    reducer.begin()

    for m in range(modes):
        middle = slice(m * window + low, m * window + high)
        back_real, back_imag = wide[middle, 0:window], wide[middle, window:]
        mid_real, mid_imag = probe[m, 0, low:high], probe[m, 1, low:high]
        grad_real += mid_real * back_real + mid_imag * back_imag
        grad_imag += mid_real * back_imag - mid_imag * back_real
    patch_grad = grad_imag * obj_real - grad_real * obj_imag
    full = exact_dot(exact_dot(place_t, patch_grad), pick_t)
    for z in range(depth):
        sent[z] = full[z : z + 1]
    copies = []
    for d in range(1, depth):
        peer = lax.rem(g + d, depth)
        copies.append(push(sent.at[peer], received.at[g], rs.at[d], rr.at[d], (a, peer)))
        copies[-1].start()
    received[g] = sent[g]
    for load in loads:
        load.wait()
    reducer.advance()
    expand(wave_small, wave)
    for copy in copies:
        copy.wait()
    total = received[0]
    for z in range(1, depth):
        total = total + received[z]
    angle_sent[:, 0:width] = total
    angle_sent[:, width:] = jnp.zeros((1, 128), F32) + number[0].astype(F32)
    copies = []
    for d in range(1, angles):
        copies.append(push(angle_sent, angle_rows.at[a], as_.at[d], ar.at[d], (lax.rem(a + d, angles), g)))
        copies[-1].start()
    angle_rows[a] = angle_sent[...]
    expand(rot_small.at[0], rot.at[0])
    reducer.advance()
    for copy in copies:
        copy.wait()

    block = width // 2
    work = []
    for c in range(2):
        cols = slice(c * block, (c + 1) * block)
        for j in range(angles):
            if c == 0:
                work.append(functools.partial(back_columns, j, angle_rows, wave, weights, rot_small, rot))
            work.append(functools.partial(back_part, j, cols, weights, rot, mix_t, wave, field))

        def finish(cols):
            out[0, :, cols] = 4.0 * dot3((fx_t[0], fx_t[1]), split(field[:, cols]))

        work.append(functools.partial(finish, cols))
    steps = 2 * reducer.stages - 2
    share = [1] * steps
    share[0] = share[-3] = 3
    share[-2], share[-1] = 4, 0
    done = 0
    for step in range(steps):
        until = -(-len(work) * sum(share[: step + 1]) // sum(share))
        for task in work[done:until]:
            task()
        done = until
        reducer.advance()
    probe_out[...] = summed[...]


def local(volume, probe, measured, angle_index, row_offset, col_offset):
    _, nx, ny = volume.shape
    modes, _, window, _ = probe.shape
    depth, angles = lax.axis_size("gz"), lax.axis_size("angle")
    rot, mix = angle_tables(nx, ny, angles)
    mix_pair = split_table(mix)
    mix_t_pair = split_table(np.swapaxes(mix, 1, 2))
    fx = packed_forward(nx)
    fx_pair, fx_t_pair = split_table(fx), split_table(fx.T)
    wave = wave_tables(ny)
    turns = 2.0 * np.pi * (np.arange(window)[:, None] * np.arange(window)[None, :] % window) / window
    cosine, sine = np.cos(turns), np.sin(turns)
    left = np.block([[cosine, sine], [-sine, cosine]])
    turn = np.stack([split_table(left), split_table(left.T)])
    big = 60 * 1024 * 1024
    hbm = pl.BlockSpec(memory_space=pl.ANY)

    row = pl.pallas_call(
        forward_kernel,
        in_specs=[SM] + [hbm] * 5,
        out_specs=VM,
        scratch_shapes=[
            pltpu.VMEM((1, nx, ny), BF16),
            pltpu.VMEM(fx_pair.shape, BF16),
            pltpu.VMEM((1,) + rot.shape[1:], F32),
            pltpu.VMEM((2, 1, ny, nx), BF16),
            pltpu.VMEM(wave.shape, F32),
            pltpu.VMEM((1, 2, nx // 2, ny), F32),
            pltpu.VMEM((2, ny // 2, ny), F32),
            pltpu.SemaphoreType.DMA((5,)),
        ],
        out_shape=jax.ShapeDtypeStruct((1, ny), F32),
        compiler_params=pltpu.CompilerParams(vmem_limit_bytes=big),
        name="forward",
    )(angle_index, volume, fx_pair, rot, mix_pair, wave)

    dma = pltpu.SemaphoreType.DMA
    block_rows = nx // angles
    tiles = modes * 2 * window // 8
    plan = reduce_plan(angles, depth, tiles)
    stages = 2 * len(plan[0][0])
    out, probe_total = pl.pallas_call(
        functools.partial(window_kernel, modes, plan),
        out_shape=(
            jax.ShapeDtypeStruct((1, block_rows, ny), F32),
            jax.ShapeDtypeStruct((tiles, 8, window), F32),
        ),
        in_specs=[SM, SM, SM, VM] + [hbm] * 7,
        out_specs=(VM, VM),
        scratch_shapes=[
            pltpu.VMEM((depth, 1, ny), F32),
            pltpu.VMEM((depth, 1, ny), F32),
            pltpu.VMEM((depth, 1, ny), F32),
            pltpu.VMEM((1, ny + 128), F32),
            pltpu.VMEM((angles, 1, ny + 128), F32),
            pltpu.VMEM((2 * window, modes * window), F32),
            pltpu.VMEM((modes * window, 2 * window), F32),
            pltpu.VMEM(probe.shape, F32),
            pltpu.VMEM(measured.shape, F32),
            pltpu.VMEM(turn.shape, BF16),
            pltpu.VMEM((2 * window, modes * window), F32),
            pltpu.VMEM((modes * 2 * depth, 2 * window), F32),
            pltpu.VMEM((angles, 2, ny // 2, 1), F32),
            pltpu.VMEM(wave.shape, F32),
            pltpu.VMEM(rot.shape, F32),
            pltpu.VMEM((2, ny // 2, ny), F32),
            pltpu.VMEM((angles, 2, nx // 2, ny), F32),
            pltpu.VMEM(mix_t_pair.shape, BF16),
            pltpu.VMEM((2, block_rows, nx), BF16),
            pltpu.VMEM((nx, ny), F32),
            pltpu.VMEM((tiles, 8, window), F32),
            pltpu.VMEM((tiles, 8, window), F32),
            pltpu.VMEM((tiles, 8, window), F32),
            dma((depth,)), dma((depth,)), dma((depth,)), dma((depth,)), dma((angles,)), dma((angles,)),
            dma((7,)), dma((stages, len(plan), 3)), dma((stages, len(plan), 3)),
        ],
        compiler_params=pltpu.CompilerParams(
            collective_id=0, has_side_effects=True, vmem_limit_bytes=48 * 1024 * 1024
        ),
        name="window",
    )(row_offset, col_offset, angle_index, row, probe, measured, turn, wave, rot, mix_t_pair, fx_t_pair)
    return (out, probe_total.reshape(probe.shape))


def solution(mesh):
    return jax.shard_map(
        local,
        mesh=mesh,
        in_specs=(
            P("gz", None, None),
            P(),
            P("angle", "gz", None, None),
            P("angle"),
            P("angle", "gz"),
            P("angle", "gz"),
        ),
        out_specs=(P("gz", "angle", None), P()),
        check_vma=False,
    )
```

```python
import functools
import math

import jax
import jax.numpy as jnp
import numpy as np
from jax import lax
from jax.experimental import pallas as pl
from jax.experimental.pallas import tpu as pltpu
from jax.sharding import PartitionSpec as P

MESH = pl.DeviceIdType.MESH
F32 = jnp.float32
BF16 = jnp.bfloat16
VM = pl.BlockSpec(memory_space=pltpu.VMEM)
SM = pl.BlockSpec(memory_space=pltpu.SMEM)


def split_table(table):
    table = np.asarray(table, np.float32)
    high = table.astype(jnp.bfloat16)
    low = (table - high.astype(np.float32)).astype(jnp.bfloat16)
    return np.stack([high, low])


def split(value):
    high = value.astype(BF16)
    return high, (value - high.astype(F32)).astype(BF16)


def dot(a, b):
    return jnp.dot(a, b, preferred_element_type=F32)


def dot3(a, b):
    return dot(a[0], b[0]) + (dot(a[0], b[1]) + dot(a[1], b[0]))


def packed_forward(n):
    k = np.arange(n // 2)[:, None]
    x = np.arange(n)[None, :]
    turns = 2.0 * np.pi * (k * x % n) / n
    imag = -np.sin(turns)
    imag[0] = np.where(x[0] % 2 == 0, 1.0, -1.0)
    return np.concatenate([np.cos(turns), imag], axis=0)


FINE = 16


def phase_table(unit, nyquist, count):
    rows = np.arange(FINE)[:, None]
    coarse = np.arange(count // 2 // FINE)[:, None] * FINE
    table = np.zeros((5, max(FINE, coarse.shape[0]), unit.shape[0]))
    for at, steps in ((0, coarse), (2, rows)):
        table[at, : len(steps)] = np.cos(steps * unit)
        table[at + 1, : len(steps)] = np.sin(steps * unit)
    table[4, 0] = nyquist
    return table.astype(np.float32)


def expand(small, full):
    fine_cos, fine_sin = small[2, 0:FINE], small[3, 0:FINE]
    for a in range(full.shape[1] // FINE):
        coarse_cos, coarse_sin = small[0, a : a + 1], small[1, a : a + 1]
        rows = slice(a * FINE, (a + 1) * FINE)
        full[0, rows] = coarse_cos * fine_cos - coarse_sin * fine_sin
        full[1, rows] = coarse_sin * fine_cos + coarse_cos * fine_sin
    full[1, 0:1] = small[4, 0:1]


def wave_tables(n):
    y = np.arange(n)
    return phase_table(2.0 * np.pi * y / n, np.where(y % 2 == 0, 1.0, -1.0), n)


def angle_tables(nx, ny, count):
    rot, mix = [], []
    cells_y = np.arange(ny)[None, :] - ny / 2
    cells_x = np.arange(nx)[None, :] - nx / 2
    weight = np.full(nx // 2, 2.0 / nx)
    weight[0] = 1.0 / nx
    for number in range(count):
        theta = math.pi * (number + 0.5) / count - math.pi / 2
        shear_x = -math.tan(theta / 2)
        shear_y = math.sin(theta)
        unit = -2.0 * np.pi * shear_x * cells_y[0] / nx
        rot.append(phase_table(unit, np.cos(unit * (nx // 2)), nx))
        ky = np.arange(ny // 2)[:, None]
        two = -2.0 * np.pi * ky * shear_y * cells_x / ny
        nyquist_two = 2.0 * np.pi * (ny // 2) * shear_y * cells_x[0] / ny
        upper, lower = np.cos(two), np.sin(two)
        lower[0] = np.cos(nyquist_two)
        spectrum = np.fft.rfft(np.concatenate([upper, lower], axis=0), axis=1)
        real = spectrum.real[:, : nx // 2] * weight
        imag = spectrum.imag[:, : nx // 2] * weight
        imag[:, 0] = spectrum.real[:, nx // 2] / nx
        mix.append(np.concatenate([real, imag], axis=1))
    return np.stack(rot), np.stack(mix)


def first_row(shape):
    return lax.broadcasted_iota(jnp.int32, shape, 0) == 0


def half_weights(n):
    return jnp.where(first_row((n // 2, 1)), 1.0 / n, 2.0 / n).astype(F32)


def forward_kernel(number, volume_hbm, fx_hbm, rot_hbm, mix_hbm, wave_hbm, out, volume, fx, rot_small, mix, wave_small, rot, wave, sems):
    angle = number[0]
    loads = [
        pltpu.make_async_copy(volume_hbm, volume, sems.at[0]),
        pltpu.make_async_copy(fx_hbm, fx, sems.at[1]),
        pltpu.make_async_copy(rot_hbm.at[pl.ds(angle, 1)], rot_small, sems.at[2]),
        pltpu.make_async_copy(mix_hbm.at[:, pl.ds(angle, 1)], mix, sems.at[3]),
        pltpu.make_async_copy(wave_hbm, wave_small, sems.at[4]),
    ]
    for at in (2, 4, 0, 1, 3):
        loads[at].start()
    n = volume.shape[1]
    half = n // 2
    loads[2].wait()
    expand(rot_small.at[0], rot.at[0])
    loads[4].wait()
    expand(wave_small, wave)
    loads[0].wait()
    loads[1].wait()
    field = volume[0]
    spec = dot(fx[0], field) + dot(fx[1], field)
    real, imag = spec[:half], spec[half:]
    top = first_row((half, 1))
    cosine, raw = rot[0, 0], rot[0, 1]
    sine = jnp.where(top, 0.0, raw)
    turned = jnp.concatenate(
        [real * cosine - imag * sine, real * sine + imag * jnp.where(top, raw, cosine)], axis=0
    )
    loads[3].wait()
    beam = dot3((mix[0, 0], mix[1, 0]), split(turned))
    upper, lower = beam[:half], beam[half:]
    cosine, raw = wave[0], wave[1]
    sine = jnp.where(top, 0.0, raw)
    weight = half_weights(wave.shape[2])
    sum_real = weight * jnp.sum(upper * cosine + lower * sine, axis=1, keepdims=True)
    sum_imag = weight * jnp.sum(
        lower * jnp.where(top, raw, cosine) - upper * sine, axis=1, keepdims=True
    )
    out[...] = jnp.sum(
        sum_real * cosine - sum_imag * jnp.where(top, -raw, raw), axis=0, keepdims=True
    )


def exact_dot(a, b):
    return jnp.dot(a, b, precision=lax.Precision.HIGHEST, preferred_element_type=F32)


def reduce_plan(angles, depth, tiles):
    core = [("gz", 1, 2)]
    along_xy = [("angle", 1, 4)] + [("angle", 1 << b, 2) for b in range(2, angles.bit_length() - 1)]
    along_z = [("gz", 2, 4)] + [("gz", 1 << b, 2) for b in range(3, depth.bit_length() - 1)]
    xy_first = core + along_xy + along_z
    z_first = core + along_z + along_xy
    unit = angles * depth
    if tiles != 8 * unit:
        return [(xy_first, tiles)]
    return [(xy_first, 3 * unit), (z_first, unit), (xy_first, 3 * unit), (z_first, unit)]


class Reducer:
    def __init__(self, place, plan, acc, land, total, sems):
        self.place, self.acc, self.land, self.total = place, acc, land, total
        self.sems = sems
        self.plan = [order for order, _ in plan]
        self.length = [size for _, size in plan]
        self.start = [sum(self.length[:i]) for i in range(len(plan))]
        self.offset = list(self.start)
        self.stages = len(self.plan[0])
        self.flying = []

    def partners(self, axis, unit, ways):
        index = self.place[axis]
        mine = lax.rem(index // unit, ways)
        found = []
        for mask in range(1, ways):
            piece = 0
            for b in range(ways.bit_length() - 1):
                bit = lax.rem(mine // (1 << b), 2)
                piece = piece + (1 << b) * (1 - bit if mask >> b & 1 else bit)
            other = dict(self.place)
            other[axis] = index + (piece - mine) * unit
            found.append((piece, (other["angle"], other["gz"])))
        return mine, found

    def copy(self, src, dst, stage, stream, lane, device):
        send, recv = self.sems
        made = pltpu.make_async_remote_copy(
            src_ref=src, dst_ref=dst, send_sem=send.at[stage, stream, lane], recv_sem=recv.at[stage, stream, lane],
            device_id=device, device_id_type=MESH,
        )
        made.start()
        return made

    def start_halving(self, stage, i):
        ways = self.plan[i][stage][2]
        mine, found = self.partners(*self.plan[i][stage])
        size = self.length[i] // ways
        made, landings = [], []
        for lane, (piece, device) in enumerate(found):
            landing = pl.ds(self.offset[i] + lane * size, size)
            other = pl.ds(self.start[i] + piece * size, size)
            made.append(self.copy(self.acc.at[other], self.land.at[landing], stage, i, lane, device))
            landings.append(landing)
        self.flying.append((made, self.start[i] + mine * size, size, landings))

    def start_doubling(self, stage, i):
        step = self.plan[i][2 * self.stages - 1 - stage]
        mine, found = self.partners(*step)
        rows = self.total.at[pl.ds(self.start[i], self.length[i])]
        made = [self.copy(rows, rows, stage, i, lane, device) for lane, (_, device) in enumerate(found)]
        self.start[i] = self.start[i] - mine * self.length[i]
        self.length[i] *= step[2]
        self.flying.append((made,))

    def begin(self):
        self.stage = 0
        for i in range(len(self.plan)):
            self.start_halving(0, i)

    def advance(self):
        flying, self.flying = self.flying, []
        after = self.stage + 1
        for i, (made, *rest) in enumerate(flying):
            for one in made:
                one.wait()
            if self.stage < self.stages:
                keep, size, landings = rest
                rows = pl.ds(keep, size)
                into = self.acc if after < self.stages else self.total
                value = self.acc[rows]
                for landing in landings:
                    value = value + self.land[landing]
                into[rows] = value
                self.start[i], self.length[i] = keep, size
                self.offset[i] += size * len(landings)
            if after < self.stages:
                self.start_halving(after, i)
            elif after < 2 * self.stages:
                self.start_doubling(after, i)
        self.stage = after


def back_columns(j, angle_rows, wave, weights, rot_small, rot):
    if j > 0:
        expand(rot_small.at[j], rot.at[j])
    half, width = wave.shape[1], wave.shape[2]
    row = jnp.zeros((1, width), F32)
    for a in range(angle_rows.shape[0]):
        mine = angle_rows[a, :, width : width + 1] == float(j)
        row = row + jnp.where(mine, angle_rows[a, :, 0:width], 0.0)
    cosine, raw = wave[0], wave[1]
    top = first_row((half, 1))
    weight = half_weights(width)
    weights[j, 0] = weight * jnp.sum(row * cosine, axis=1, keepdims=True)
    weights[j, 1] = -weight * jnp.sum(row * jnp.where(top, -raw, raw), axis=1, keepdims=True)


def back_part(j, cols, weights, rot, mix_t, wave, acc):
    in_real, in_imag = weights[j, 0], weights[j, 1]
    cosine, raw = wave[0, :, cols], wave[1, :, cols]
    top = first_row((cosine.shape[0], 1))
    sine = jnp.where(top, 0.0, raw)
    beam = jnp.concatenate(
        [in_real * cosine - in_imag * sine, in_real * sine + in_imag * jnp.where(top, raw, cosine)], axis=0
    )
    turned = dot3((mix_t[0, j], mix_t[1, j]), split(beam))
    kx = turned.shape[0] // 2
    real, imag = turned[:kx], turned[kx:]
    top = first_row((kx, 1))
    cosine, raw = rot[j, 0, :, cols], rot[j, 1, :, cols]
    sine = jnp.where(top, 0.0, raw)
    upper = real * cosine + imag * sine
    lower = imag * jnp.where(top, raw, cosine) - real * sine
    if j > 0:
        upper, lower = acc[:kx, cols] + upper, acc[kx:, cols] + lower
    acc[:kx, cols] = upper
    acc[kx:, cols] = lower


def window_kernel(
    modes, plan, row_off, col_off, number, row, probe_hbm, measured_hbm, turn_hbm, wave_hbm, rot_hbm, mix_hbm, fx_hbm,
    out, probe_out,
    gathered, sent, received, angle_sent, angle_rows, mat, wide, probe, measured, turn, base, thin, weights, wave_small, rot_small,
    wave, rot, mix_t, fx_t, field, acc, land, summed,
    gs, gr, rs, rr, as_, ar, tables, reduce_send, reduce_recv,
):
    depth, angles = gathered.shape[0], angle_rows.shape[0]
    width = row.shape[1]
    window = probe.shape[-1]
    half = window // 2
    g, a = lax.axis_index("gz"), lax.axis_index("angle")

    block_rows = fx_t.shape[1]
    early = [
        pltpu.make_async_copy(turn_hbm, turn, tables.at[4]),
        pltpu.make_async_copy(probe_hbm, probe, tables.at[5]),
        pltpu.make_async_copy(measured_hbm, measured, tables.at[6]),
    ]
    for load in early:
        load.start()
    loads = [
        pltpu.make_async_copy(wave_hbm, wave_small, tables.at[0]),
        pltpu.make_async_copy(rot_hbm, rot_small, tables.at[1]),
        pltpu.make_async_copy(mix_hbm, mix_t, tables.at[2]),
        pltpu.make_async_copy(fx_hbm.at[:, pl.ds(a * block_rows, block_rows)], fx_t, tables.at[3]),
    ]
    barrier = pltpu.get_barrier_semaphore()
    for d in range(1, depth):
        pl.semaphore_signal(barrier, inc=1, device_id=(a, lax.rem(g + d, depth)), device_id_type=MESH)
    for d in range(1, angles):
        pl.semaphore_signal(barrier, inc=1, device_id=(lax.rem(a + d, angles), g), device_id_type=MESH)
    pl.semaphore_wait(barrier, depth + angles - 2)

    def push(src, dst, send, recv, device):
        return pltpu.make_async_remote_copy(
            src_ref=src, dst_ref=dst, send_sem=send, recv_sem=recv, device_id=device, device_id_type=MESH
        )

    copies = []
    for d in range(1, depth):
        copies.append(push(row, gathered.at[g], gs.at[d], gr.at[d], (a, lax.rem(g + d, depth))))
        copies[-1].start()
    gathered[g] = row[...]
    for load in early:
        load.wait()
    for load in loads:
        load.start()

    row0, col0 = row_off[0, 0], col_off[0, 0]
    iota = lax.broadcasted_iota
    pick = (iota(jnp.int32, (width, window), 0) == iota(jnp.int32, (width, window), 1) + col0).astype(F32)
    pick_t = (iota(jnp.int32, (window, width), 1) == iota(jnp.int32, (window, width), 0) + col0).astype(F32)
    shape = (2 * depth, depth)
    place = (
        iota(jnp.int32, shape, 0) + (half - depth) == iota(jnp.int32, shape, 1) - row0
    ).astype(F32)
    place_t = (
        iota(jnp.int32, shape[::-1], 1) + (half - depth) == iota(jnp.int32, shape[::-1], 0) - row0
    ).astype(F32)
    low, high, band = half - depth, half + depth, 2 * depth
    left, left_t = (turn[0, 0], turn[0, 1]), (turn[1, 0], turn[1, 1])

    def lanes(m):
        return slice(m * window, (m + 1) * window)

    for m in range(modes):
        wide[lanes(m), 0:window] = probe[m, 0]
        wide[lanes(m), window:] = probe[m, 1]
    wide[...] = dot3(split(wide[...]), left_t)
    for m in range(modes):
        mat[0:window, lanes(m)] = wide[lanes(m), 0:window]
        mat[window:, lanes(m)] = wide[lanes(m), window:]
    base[...] = dot3(left, split(mat[...]))
    for copy in copies:
        copy.wait()

    rows = jnp.concatenate([gathered[z] for z in range(depth)], axis=0)
    patch = exact_dot(place, exact_dot(rows, pick))
    obj_real, obj_imag = jnp.cos(patch), jnp.sin(patch)
    for m in range(modes):
        mid_real, mid_imag = probe[m, 0, low:high], probe[m, 1, low:high]
        thin[m * band : (m + 1) * band, 0:window] = mid_real * obj_real - mid_imag * obj_imag - mid_real
        thin[m * band : (m + 1) * band, window:] = mid_real * obj_imag + mid_imag * obj_real - mid_imag
    change = dot3(split(thin[...]), left_t)
    change = jnp.concatenate(
        [
            jnp.concatenate([change[m * band : (m + 1) * band, c : c + window] for m in range(modes)], axis=1)
            for c in (0, window)
        ],
        axis=0,
    )
    near = tuple(
        jnp.concatenate([part[:, low:high], part[:, window + low : window + high]], axis=1) for part in left
    )
    mat[...] = base[...] + dot3(near, split(change))
    intensity = jnp.zeros((window, window), F32)
    for m in range(modes):
        far_real, far_imag = mat[0:window, lanes(m)], mat[window:, lanes(m)]
        intensity += far_real * far_real + far_imag * far_imag
    factor = (1.0 - jnp.sqrt(measured[0, 0] + 1.0) / jnp.sqrt(intensity + 1.0)) / window
    for m in range(modes):
        mat[0:window, lanes(m)] = mat[0:window, lanes(m)] * factor
        mat[window:, lanes(m)] = mat[window:, lanes(m)] * factor
    mat[...] = dot3(left_t, split(mat[...]))
    for m in range(modes):
        wide[lanes(m), 0:window] = mat[0:window, lanes(m)]
        wide[lanes(m), window:] = mat[window:, lanes(m)]
    wide[...] = dot3(split(wide[...]), left)

    tiles = window // 8
    shape = (tiles, 8, window)
    part = (depth // 4, 8, window)
    grad_real = jnp.zeros((band, window), F32)
    grad_imag = jnp.zeros((band, window), F32)
    for m in range(modes):
        first = m * window
        at = 2 * m * tiles
        acc[at : at + tiles] = wide[lanes(m), 0:window].reshape(shape) * 0.0625
        acc[at + tiles : at + 2 * tiles] = wide[lanes(m), window:].reshape(shape) * 0.0625
        middle = slice(first + low, first + high)
        back_real, back_imag = wide[middle, 0:window], wide[middle, window:]
        top_tile, end_tile = at + low // 8, at + high // 8
        acc[top_tile:end_tile] = (obj_real * back_real + obj_imag * back_imag).reshape(part) * 0.0625
        acc[top_tile + tiles : end_tile + tiles] = (
            obj_real * back_imag - obj_imag * back_real
        ).reshape(part) * 0.0625
    reducer = Reducer({"angle": a, "gz": g}, plan, acc, land, summed, (reduce_send, reduce_recv))
    reducer.begin()

    for m in range(modes):
        middle = slice(m * window + low, m * window + high)
        back_real, back_imag = wide[middle, 0:window], wide[middle, window:]
        mid_real, mid_imag = probe[m, 0, low:high], probe[m, 1, low:high]
        grad_real += mid_real * back_real + mid_imag * back_imag
        grad_imag += mid_real * back_imag - mid_imag * back_real
    patch_grad = grad_imag * obj_real - grad_real * obj_imag
    full = exact_dot(exact_dot(place_t, patch_grad), pick_t)
    for z in range(depth):
        sent[z] = full[z : z + 1]
    copies = []
    for d in range(1, depth):
        peer = lax.rem(g + d, depth)
        copies.append(push(sent.at[peer], received.at[g], rs.at[d], rr.at[d], (a, peer)))
        copies[-1].start()
    received[g] = sent[g]
    for load in loads:
        load.wait()
    reducer.advance()
    expand(wave_small, wave)
    for copy in copies:
        copy.wait()
    total = received[0]
    for z in range(1, depth):
        total = total + received[z]
    angle_sent[:, 0:width] = total
    angle_sent[:, width:] = jnp.zeros((1, 128), F32) + number[0].astype(F32)
    copies = []
    for d in range(1, angles):
        copies.append(push(angle_sent, angle_rows.at[a], as_.at[d], ar.at[d], (lax.rem(a + d, angles), g)))
        copies[-1].start()
    angle_rows[a] = angle_sent[...]
    expand(rot_small.at[0], rot.at[0])
    reducer.advance()
    for copy in copies:
        copy.wait()

    block = width // 2
    work = []
    for c in range(2):
        cols = slice(c * block, (c + 1) * block)
        for j in range(angles):
            if c == 0:
                work.append(functools.partial(back_columns, j, angle_rows, wave, weights, rot_small, rot))
            work.append(functools.partial(back_part, j, cols, weights, rot, mix_t, wave, field))

        def finish(cols):
            out[0, :, cols] = 4.0 * dot3((fx_t[0], fx_t[1]), split(field[:, cols]))

        work.append(functools.partial(finish, cols))
    steps = 2 * reducer.stages - 2
    share = [1] * steps
    share[0] = share[-3] = 3
    share[-2], share[-1] = 4, 0
    done = 0
    for step in range(steps):
        until = -(-len(work) * sum(share[: step + 1]) // sum(share))
        for task in work[done:until]:
            task()
        done = until
        reducer.advance()
    probe_out[...] = summed[...]


def local(volume, probe, measured, angle_index, row_offset, col_offset):
    _, nx, ny = volume.shape
    modes, _, window, _ = probe.shape
    depth, angles = lax.axis_size("gz"), lax.axis_size("angle")
    rot, mix = angle_tables(nx, ny, angles)
    mix_pair = split_table(mix)
    mix_t_pair = split_table(np.swapaxes(mix, 1, 2))
    fx = packed_forward(nx)
    fx_pair, fx_t_pair = split_table(fx), split_table(fx.T)
    wave = wave_tables(ny)
    turns = 2.0 * np.pi * (np.arange(window)[:, None] * np.arange(window)[None, :] % window) / window
    cosine, sine = np.cos(turns), np.sin(turns)
    left = np.block([[cosine, sine], [-sine, cosine]])
    turn = np.stack([split_table(left), split_table(left.T)])
    big = 60 * 1024 * 1024
    hbm = pl.BlockSpec(memory_space=pl.ANY)

    row = pl.pallas_call(
        forward_kernel,
        in_specs=[SM] + [hbm] * 5,
        out_specs=VM,
        scratch_shapes=[
            pltpu.VMEM((1, nx, ny), BF16),
            pltpu.VMEM(fx_pair.shape, BF16),
            pltpu.VMEM((1,) + rot.shape[1:], F32),
            pltpu.VMEM((2, 1, ny, nx), BF16),
            pltpu.VMEM(wave.shape, F32),
            pltpu.VMEM((1, 2, nx // 2, ny), F32),
            pltpu.VMEM((2, ny // 2, ny), F32),
            pltpu.SemaphoreType.DMA((5,)),
        ],
        out_shape=jax.ShapeDtypeStruct((1, ny), F32),
        compiler_params=pltpu.CompilerParams(vmem_limit_bytes=big),
        name="forward",
    )(angle_index, volume, fx_pair, rot, mix_pair, wave)

    dma = pltpu.SemaphoreType.DMA
    block_rows = nx // angles
    tiles = modes * 2 * window // 8
    plan = reduce_plan(angles, depth, tiles)
    stages = 2 * len(plan[0][0])
    out, probe_total = pl.pallas_call(
        functools.partial(window_kernel, modes, plan),
        out_shape=(
            jax.ShapeDtypeStruct((1, block_rows, ny), F32),
            jax.ShapeDtypeStruct((tiles, 8, window), F32),
        ),
        in_specs=[SM, SM, SM, VM] + [hbm] * 7,
        out_specs=(VM, VM),
        scratch_shapes=[
            pltpu.VMEM((depth, 1, ny), F32),
            pltpu.VMEM((depth, 1, ny), F32),
            pltpu.VMEM((depth, 1, ny), F32),
            pltpu.VMEM((1, ny + 128), F32),
            pltpu.VMEM((angles, 1, ny + 128), F32),
            pltpu.VMEM((2 * window, modes * window), F32),
            pltpu.VMEM((modes * window, 2 * window), F32),
            pltpu.VMEM(probe.shape, F32),
            pltpu.VMEM(measured.shape, F32),
            pltpu.VMEM(turn.shape, BF16),
            pltpu.VMEM((2 * window, modes * window), F32),
            pltpu.VMEM((modes * 2 * depth, 2 * window), F32),
            pltpu.VMEM((angles, 2, ny // 2, 1), F32),
            pltpu.VMEM(wave.shape, F32),
            pltpu.VMEM(rot.shape, F32),
            pltpu.VMEM((2, ny // 2, ny), F32),
            pltpu.VMEM((angles, 2, nx // 2, ny), F32),
            pltpu.VMEM(mix_t_pair.shape, BF16),
            pltpu.VMEM((2, block_rows, nx), BF16),
            pltpu.VMEM((nx, ny), F32),
            pltpu.VMEM((tiles, 8, window), F32),
            pltpu.VMEM((tiles, 8, window), F32),
            pltpu.VMEM((tiles, 8, window), F32),
            dma((depth,)), dma((depth,)), dma((depth,)), dma((depth,)), dma((angles,)), dma((angles,)),
            dma((7,)), dma((stages, len(plan), 3)), dma((stages, len(plan), 3)),
        ],
        compiler_params=pltpu.CompilerParams(
            collective_id=0, has_side_effects=True, vmem_limit_bytes=48 * 1024 * 1024
        ),
        name="window",
    )(row_offset, col_offset, angle_index, row, probe, measured, turn, wave, rot, mix_t_pair, fx_t_pair)
    return (out, probe_total.reshape(probe.shape))


def solution(mesh):
    return jax.shard_map(
        local,
        mesh=mesh,
        in_specs=(
            P("gz", None, None),
            P(),
            P("angle", "gz", None, None),
            P("angle"),
            P("angle", "gz"),
            P("angle", "gz"),
        ),
        out_specs=(P("gz", "angle", None), P()),
        check_vma=False,
    )
```
